128 devices in a mesh: ctx: 16 (over x, z), head: 8 (over y, core).
Axes of the slice: x: 4, y: 4, z: 4, core: 2. Of those that a mesh axis runs over, the one named last changes fastest.
Arguments:
- x_tokens: bfloat16 [16384, 16384], P('ctx', 'head'), may hold values from -6 to 6
- bc_tokens: bfloat16 [16384, 2, 8, 256], P('ctx', None, 'head'), may hold values from -6 to 6
- z_tokens: bfloat16 [16384, 16384], P('ctx', 'head'), may hold values from -6 to 6
- dt_tokens: float32 [16384, 256], P('ctx', 'head'), may hold values from -3.5 to 16384
- conv_x: bfloat16 [4, 16384], P(None, 'head'), may hold values from -3 to 3
- conv_bc: bfloat16 [4, 2, 8, 256], P(None, None, 'head'), may hold values from -3 to 3
- bias_x: bfloat16 [16384], P('head'), may hold values from -0.75 to -0.25
- bias_bc: bfloat16 [2, 8, 256], P(None, 'head'), may hold values from -3 to 3
- a_log: float32 [256], replicated, may hold values from -12 to 3
- dt_bias: float32 [256], replicated, may hold values from -5 to -2.9
- d_skip: float32 [256], replicated, may hold values from 0.5 to 1.5
- norm_gain: float32 [16384], replicated, may hold values from 0.5 to 1.5
- state_cache: bfloat16 [32, 256, 64, 256], P(None, ('ctx', 'head')), may hold values from -6 to 6
- traj_slot: int32 [32], replicated, may hold values from 0 to 31, each once
- row_traj: int32 [128], replicated, may hold values from 0 to 31, as said below
- x_decode: bfloat16 [4, 128, 16384], P(None, None, ('ctx', 'head')), may hold values from -20 to 20
- bc_decode: bfloat16 [4, 128, 2, 8, 256], replicated, may hold values from -6 to 6
- z_decode: bfloat16 [4, 128, 16384], P(None, None, ('ctx', 'head')), may hold values from -6 to 6
- dt_decode: float32 [4, 128, 256], P(None, None, ('ctx', 'head')), may hold values from -3 to 3
Outputs:
- prefill_out: bfloat16 [16384, 16384], P('ctx', 'head')
- decode_out: bfloat16 [4, 128, 16384], P(None, None, ('ctx', 'head'))
The draws below stay inside these ranges and needn't reach their ends.
Inputs may be any that keep to these rules, and one draw needn't show every extreme that they name: `traj_slot`: each of the 32 slots once. `row_traj`: each trajectory is named by exactly 4 rows.
All inputs are finite; a program needn't handle non-finite values.
Results may differ from the reference program's by a relative error of at most 0.011.
Values may be sent and summed in bfloat16 or wider, within the bound.
No kernel may reach another device: no remote copies, remote signals or barrier semaphores. Data moves between devices by JAX's collectives and lax.ppermute only.
A program may use at most 384 MiB of HBM per device.

```python
from functools import partial
import jax
import jax.numpy as jnp
from jax import lax

HEADS = 256
P_SIZE = 64
N = 256
NGROUPS = 8
K = 4
BLOCK = 128
SLOTS = 32
STEPS = 4
APPENDED_LENGTH = 16384
ROWS = 128


def head_rates(key, slow_share):
    random_key_series = jax.random.split(key, 4)
    slow_mask = jax.random.uniform(random_key_series[0], (HEADS,)) < slow_share
    base_dt = jnp.exp(jax.random.uniform(random_key_series[1], (HEADS,), minval=jnp.log(0.01), maxval=jnp.log(0.05)))
    fast_rate = jnp.exp(jax.random.uniform(random_key_series[2], (HEADS,), minval=jnp.log(0.02), maxval=jnp.log(0.1)))
    slow_rate = jnp.exp(jax.random.uniform(random_key_series[3], (HEADS,), minval=jnp.log(0.3), maxval=jnp.log(2.0))) / APPENDED_LENGTH
    return (base_dt, jnp.where(slow_mask, slow_rate, fast_rate) / base_dt)


def surge_layout(key, decay_factor):
    random_key_series = jax.random.split(jax.random.fold_in(key, 91), 2)
    surge_token_rows = jax.random.randint(random_key_series[0], (3,), 0, APPENDED_LENGTH)
    dropped_fraction = jax.random.uniform(random_key_series[1], (3, 1), minval=0.2, maxval=0.5)
    return (surge_token_rows, -jnp.log(1.0 - dropped_fraction) / decay_factor[None, :])


def draw_a_log(key, part):
    slow_share = 0.5
    base_dt, decay_factor = head_rates(key, slow_share)
    return jnp.log(decay_factor).astype(jnp.float32)


def draw_dt_bias(key, part):
    slow_share = 0.5
    base_dt, decay_factor = head_rates(key, slow_share)
    return jnp.log(jnp.expm1(base_dt)).astype(jnp.float32)


def draw_dt_tokens(key, part):
    slow_share = 0.5
    base_dt, decay_factor = head_rates(key, slow_share)
    surge_token_rows, target_step_size = surge_layout(key, decay_factor)
    own_key = jax.random.fold_in(key, 5)
    value_entries = 0.5 * jnp.clip(jax.random.normal(own_key, (APPENDED_LENGTH, HEADS)), -6.0, 6.0)
    raised_values = target_step_size + jnp.log(-jnp.expm1(-target_step_size)) - jnp.log(jnp.expm1(base_dt))[None, :]
    token_positions = jnp.arange(APPENDED_LENGTH)
    for surge_position in range(3):
        value_entries = jnp.where((token_positions == surge_token_rows[surge_position])[:, None], raised_values[surge_position][None, :], value_entries)
    return value_entries.astype(jnp.float32)


def draw_x_tokens(key, part):
    slow_share = 0.5
    base_dt, decay_factor = head_rates(key, slow_share)
    surge_token_rows, target_step_size = surge_layout(key, decay_factor)
    own_key = jax.random.fold_in(key, 7)
    value_entries = jnp.clip(jax.random.normal(own_key, (APPENDED_LENGTH, HEADS, P_SIZE)), -6.0, 6.0)
    shrink_factor = jnp.minimum(1.0, base_dt[None, :] / target_step_size)
    token_positions = jnp.arange(APPENDED_LENGTH)
    for surge_position in range(3):
        value_entries = jnp.where((token_positions == surge_token_rows[surge_position])[:, None, None], value_entries * shrink_factor[surge_position][None, :, None], value_entries)
    return value_entries.reshape(APPENDED_LENGTH, HEADS * P_SIZE).astype(jnp.bfloat16)


def draw_bias_x(key, part):
    key = jax.random.fold_in(key, 23)
    value_entries = jax.random.uniform(key, (HEADS * P_SIZE,), minval=-0.75, maxval=-0.25)
    return value_entries.astype(jnp.bfloat16)


def draw_bias_bc(key, part):
    key = jax.random.fold_in(key, 29)
    random_key_series = jax.random.split(key, 2)
    b_half = jax.random.uniform(random_key_series[0], (NGROUPS, N), minval=-0.75, maxval=-0.25)
    c_half = 0.5 * jnp.clip(jax.random.normal(random_key_series[1], (NGROUPS, N)), -6.0, 6.0)
    return jnp.stack([b_half, c_half]).astype(jnp.bfloat16)


def draw_row_traj(key, part):
    key = jax.random.fold_in(key, 11)
    base_ids = jnp.arange(ROWS, dtype=jnp.int32) % SLOTS
    order = jax.random.permutation(key, ROWS)
    return base_ids[order].astype(jnp.int32)


def draw_x_decode(key, part):
    key = jax.random.fold_in(key, 17)
    random_key_series = jax.random.split(key, 2)
    value_entries = jnp.clip(jax.random.normal(random_key_series[0], (STEPS, ROWS, HEADS * P_SIZE)), -6.0, 6.0)
    column = jnp.arange(HEADS * P_SIZE, dtype=jnp.float32) / (HEADS * P_SIZE)
    spread = jnp.exp(jnp.log(3.0) * column + jax.random.uniform(random_key_series[1], (HEADS * P_SIZE,), minval=0.0, maxval=jnp.log(3.0)))
    return (0.3 * value_entries * spread).astype(jnp.bfloat16)


def shard_levels(key, dims, cuts, least, high):
    gain = 1.0
    for dim, blocks in cuts:
        heights = jax.random.uniform(jax.random.fold_in(jax.random.fold_in(key, 6), dim), (blocks,), jnp.float32, least / len(cuts), high / len(cuts))
        gain = gain * jnp.repeat(jnp.exp(heights), dims[dim] // blocks).reshape((-1,) + (1,) * (len(dims) - 1 - dim))
    return gain


def gaussian(rng, extent, scale, bound, shards=(), held_as=jnp.bfloat16):
    gain = shard_levels(rng, extent, shards, -0.22, 0.18) if shards else 1.0
    drawn = jax.random.normal(rng, extent, jnp.float32) * scale * gain
    return jnp.minimum(jnp.maximum(drawn, -bound), bound).astype(held_as)


def setup_inputs(seed: int = 0) -> dict:
    streams_of = jax.random.split(jax.random.key(seed), 20)
    return {
        "x_tokens": draw_x_tokens(jax.random.fold_in(streams_of[19], 71), 0),
        "bc_tokens": gaussian(streams_of[1], (APPENDED_LENGTH, 2, NGROUPS, N), 1.0, 6.0, ((0, 16), (2, 8))),
        "z_tokens": gaussian(streams_of[2], (APPENDED_LENGTH, HEADS * P_SIZE), 1.0, 6.0, ((0, 16), (1, 8))),
        "dt_tokens": draw_dt_tokens(jax.random.fold_in(streams_of[19], 71), 0),
        "conv_x": gaussian(streams_of[4], (K, HEADS * P_SIZE), K ** -0.5, 3.0, ((1, 8),)),
        "conv_bc": gaussian(streams_of[5], (K, 2, NGROUPS, N), K ** -0.5, 3.0, ((2, 8),)),
        "bias_x": draw_bias_x(jax.random.fold_in(streams_of[19], 71), 0),
        "bias_bc": draw_bias_bc(jax.random.fold_in(streams_of[19], 71), 0),
        "a_log": draw_a_log(jax.random.fold_in(streams_of[19], 71), 0),
        "dt_bias": draw_dt_bias(jax.random.fold_in(streams_of[19], 71), 0),
        "d_skip": jnp.clip(jax.random.uniform(streams_of[10], (HEADS,), jnp.float32, 0.5, 1.5), 0.5, 1.5),
        "norm_gain": jnp.clip(1.0 + 0.1 * jax.random.normal(streams_of[11], (HEADS * P_SIZE,), jnp.float32), 0.5, 1.5),
        "state_cache": gaussian(streams_of[12], (SLOTS, HEADS, P_SIZE, N), 1.0, 6.0, ((1, 128),)),
        "traj_slot": jax.random.permutation(streams_of[13], SLOTS).astype(jnp.int32),
        "row_traj": draw_row_traj(jax.random.fold_in(streams_of[19], 71), 0),
        "x_decode": draw_x_decode(jax.random.fold_in(streams_of[19], 71), 0),
        "bc_decode": gaussian(streams_of[16], (STEPS, ROWS, 2, NGROUPS, N), 1.0, 6.0),
        "z_decode": gaussian(streams_of[17], (STEPS, ROWS, HEADS * P_SIZE), 1.0, 6.0, ((2, 128),)),
        "dt_decode": gaussian(streams_of[18], (STEPS, ROWS, HEADS), 0.5, 3.0, ((2, 128),), jnp.float32),
    }


EPSILON = 1e-05
HIGHEST = lax.Precision.HIGHEST

def rounded(value_entries):
    return lax.optimization_barrier(value_entries.astype(jnp.bfloat16))

def causal_conv(value_entries, weight, offset):
    length = value_entries.shape[0]
    padded = jnp.concatenate([jnp.zeros((K - 1,) + value_entries.shape[1:], value_entries.dtype), value_entries], 0)
    total_sum = jnp.zeros(value_entries.shape, jnp.float32) + offset.astype(jnp.float32)
    for tap_at in range(K):
        total_sum = total_sum + weight[tap_at].astype(jnp.float32) * padded[tap_at:tap_at + length].astype(jnp.float32)
    return jax.nn.silu(total_sum).astype(jnp.bfloat16)

def gated_norm(output, gate, gain_row):
    mixed_out = output * jax.nn.silu(gate.astype(jnp.float32))
    mean_sq = lax.optimization_barrier(jnp.mean(mixed_out * mixed_out, axis=-1, keepdims=True))
    return (mixed_out * lax.rsqrt(mean_sq + EPSILON) * gain_row).astype(jnp.bfloat16)

def scan_block(skip_grid, ssm_state, block):
    x_blk, b_blk, c_blk, dt_blk, log_blk = block
    running = jnp.cumsum(log_blk, axis=0)
    along_time = jnp.transpose(running, (1, 2, 0))
    dt_along = jnp.transpose(dt_blk, (1, 2, 0))
    scores = jnp.einsum('tgn,sgn->gts', c_blk.astype(jnp.float32), b_blk.astype(jnp.float32), precision=HIGHEST)
    length = along_time.shape[-1]
    causal = jnp.arange(length)[:, None] >= jnp.arange(length)[None, :]
    log_gaps = jnp.where(causal, along_time[..., :, None] - along_time[..., None, :], -jnp.inf)
    weights = rounded(jnp.exp(log_gaps) * dt_along[..., None, :] * scores[:, None])
    inner_out = jnp.einsum('ghts,sghp->tghp', weights.astype(jnp.float32), x_blk.astype(jnp.float32), precision=HIGHEST)
    tail_weight = jnp.exp(running[-1:] - running) * dt_blk
    carried = rounded(x_blk.astype(jnp.float32) * tail_weight[..., None])
    fresh_state = jnp.einsum('sghp,sgn->ghpn', carried.astype(jnp.float32), b_blk.astype(jnp.float32), precision=HIGHEST)
    state_low = rounded(ssm_state).astype(jnp.float32)
    outer_out = jnp.exp(running)[..., None] * jnp.einsum('tgn,ghpn->tghp', c_blk.astype(jnp.float32), state_low, precision=HIGHEST)
    output = inner_out + outer_out + skip_grid[..., None] * x_blk.astype(jnp.float32)
    leaving = jnp.exp(running[-1])[..., None, None] * ssm_state + fresh_state
    return (leaving, output)

def reference(x_tokens, bc_tokens, z_tokens, dt_tokens, conv_x, conv_bc, bias_x, bias_bc, a_log, dt_bias, d_skip, norm_gain, state_cache, traj_slot, row_traj, x_decode, bc_decode, z_decode, dt_decode):
    group_heads = HEADS // NGROUPS
    blocks = APPENDED_LENGTH // BLOCK
    x_conv = causal_conv(x_tokens, conv_x, bias_x)
    bc_conv = causal_conv(bc_tokens, conv_bc, bias_bc)
    decay_all = -jnp.exp(a_log)
    dt_all = jax.nn.softplus(dt_tokens + dt_bias)
    log_all = dt_all * decay_all
    initial = state_cache[traj_slot[0]].astype(jnp.float32).reshape(NGROUPS, group_heads, P_SIZE, N)
    x_blocks = x_conv.reshape(blocks, BLOCK, NGROUPS, group_heads, P_SIZE)
    b_blocks = bc_conv[:, 0].reshape(blocks, BLOCK, NGROUPS, N)
    c_blocks = bc_conv[:, 1].reshape(blocks, BLOCK, NGROUPS, N)
    dt_blocks = dt_all.reshape(blocks, BLOCK, NGROUPS, group_heads)
    log_blocks = log_all.reshape(blocks, BLOCK, NGROUPS, group_heads)
    skip_grid = d_skip.reshape(NGROUPS, group_heads)
    final_state, outputs = lax.scan(partial(scan_block, skip_grid), initial, (x_blocks, b_blocks, c_blocks, dt_blocks, log_blocks))
    outputs = outputs.reshape(APPENDED_LENGTH, NGROUPS, group_heads * P_SIZE)
    prefill_out = gated_norm(outputs, z_tokens.reshape(APPENDED_LENGTH, NGROUPS, group_heads * P_SIZE), norm_gain.reshape(NGROUPS, group_heads * P_SIZE)).reshape(APPENDED_LENGTH, HEADS * P_SIZE)

    def decode_group(inputs):
        group_at, final_group = inputs
        first_head = group_at * group_heads
        cache_group = lax.dynamic_slice_in_dim(state_cache, first_head, group_heads, 1)
        cached = cache_group[traj_slot[row_traj]].astype(jnp.float32)
        ssm_state = jnp.where((row_traj == 0)[:, None, None, None], final_group[None], cached)
        decay_g = lax.dynamic_slice_in_dim(decay_all, first_head, group_heads, 0)
        bias_g = lax.dynamic_slice_in_dim(dt_bias, first_head, group_heads, 0)
        skip_g = lax.dynamic_slice_in_dim(d_skip, first_head, group_heads, 0)
        gain_g = lax.dynamic_slice_in_dim(norm_gain, first_head * P_SIZE, group_heads * P_SIZE, 0)
        x_g = lax.dynamic_slice_in_dim(x_decode, first_head * P_SIZE, group_heads * P_SIZE, 2)
        z_g = lax.dynamic_slice_in_dim(z_decode, first_head * P_SIZE, group_heads * P_SIZE, 2)
        dt_g = lax.dynamic_slice_in_dim(dt_decode, first_head, group_heads, 2)
        bc_g = lax.dynamic_index_in_dim(bc_decode, group_at, 3, keepdims=False).astype(jnp.float32)
        results = []
        for step_at in range(STEPS):
            dt_now = jax.nn.softplus(dt_g[step_at] + bias_g)
            x_now = x_g[step_at].reshape(ROWS, group_heads, P_SIZE).astype(jnp.float32)
            ssm_state = jnp.exp(dt_now * decay_g)[:, :, None, None] * ssm_state + (dt_now[:, :, None] * x_now)[..., None] * bc_g[step_at, :, 0][:, None, None, :]
            output = jnp.einsum('rhpn,rn->rhp', ssm_state, bc_g[step_at, :, 1], precision=HIGHEST) + skip_g[:, None] * x_now
            results.append(gated_norm(output.reshape(ROWS, group_heads * P_SIZE), z_g[step_at], gain_g))
        return jnp.stack(results)
    per_group = lax.map(decode_group, (jnp.arange(NGROUPS, dtype=jnp.int32), final_state))
    decode_out = jnp.transpose(per_group, (1, 2, 0, 3)).reshape(STEPS, ROWS, HEADS * P_SIZE)
    return (prefill_out, decode_out)
```

```python
import jax
import jax.numpy as jnp
from jax import lax
from jax.experimental import pallas as pl
from jax.experimental.pallas import tpu as pltpu
from jax.sharding import PartitionSpec as P

BLOCK = 128
HEAD = 64
STATE = 256
SPAN = 32
WIDTH = SPAN * HEAD
RANKS = 16
ROWS = 128
STEPS = 4
QUAD = 256
EPSILON = 1e-05
LOG2E = 1.4426950408889634
F32 = jnp.float32
BF16 = jnp.bfloat16


def dot(a, b, dims=((1,), (0,))):
    return lax.dot_general(a, b, (dims, ((), ())), preferred_element_type=F32)


def halves(v):
    hi = v.astype(BF16)
    return hi, (v - hi.astype(F32)).astype(BF16)


def thirds(v):
    hi, mid = halves(v)
    return hi, mid, (v - hi.astype(F32) - mid.astype(F32)).astype(BF16)


def softplus(v):
    return jnp.maximum(v, 0.0) + jnp.log1p(jnp.exp(-jnp.abs(v)))


def silu(v):
    h = 0.5 * v
    return h + h * jnp.tanh(h)


def iota(shape, dim):
    return lax.broadcasted_iota(jnp.int32, shape, dim)


def fill_expander(ref):
    shape = (2 * SPAN, WIDTH)
    ref[...] = jnp.where(iota(shape, 1) // HEAD == iota(shape, 0) % SPAN, 1.0, 0.0).astype(BF16)


def conv(block, before, taps):
    joined = jnp.concatenate([before, block], 0)
    h = taps[4:5] + taps[0:1] * pltpu.roll(joined, 3, 0)[8:]
    h = h + taps[1:2] * pltpu.roll(joined, 2, 0)[8:]
    h = h + taps[2:3] * pltpu.roll(joined, 1, 0)[8:]
    h = h + taps[3:4] * block
    return (h + h * jnp.tanh(h)).astype(BF16)


def own_heads(head_at, alog_ref, bias_ref, skip_ref):
    rows = jnp.concatenate([alog_ref[...], bias_ref[...]] + [skip_ref[...]] * 6, 0)
    shape = (SPAN, rows.shape[1])
    mine = jnp.where(iota(shape, 1) == iota(shape, 0) + head_at * SPAN, 1.0, 0.0).astype(BF16)
    return sum(dot(mine, piece, ((1,), (1,))) for piece in thirds(rows))


def spread_heads(rows, spread):
    return dot(rows, spread)


def pair_halves(rows):
    return jnp.concatenate(halves(rows), 1)


def prep_kernel(at_ref, x_ref, bc_ref, edge_ref, dt_ref, alog_ref, bias_ref, skip_ref, cw_ref, cb_ref,
                bw_ref, bb_ref, xc_ref, car_ref, bco_ref, rdt_ref, send_ref,
                prevx, prevbc, state, rc, spread, own, wx, wbc):
    block_at = pl.program_id(0)

    @pl.when(block_at == 0)
    def _():
        fill_expander(spread)
        own[...] = own_heads(at_ref[0], alog_ref, bias_ref, skip_ref)
        state[...] = jnp.zeros_like(state)
        rc[...] = jnp.zeros_like(rc)
        prevx[...] = jnp.zeros_like(prevx)
        prevbc[...] = jnp.zeros_like(prevbc)
        edge = edge_ref[...].astype(F32)
        prevx[5:8, :] = edge[:, :WIDTH]
        prevbc[5:8, :] = edge[:, WIDTH:]
        wx[0:4, :] = cw_ref[...].astype(F32) * 0.5
        offset = cb_ref[...].astype(F32) * 0.5
        for i in range(WIDTH // 128):
            wx[4:5, i * 128:(i + 1) * 128] = offset[i:i + 1]
        taps = bw_ref[...].astype(F32) * 0.5
        offset = bb_ref[...].astype(F32) * 0.5
        for i in range(2):
            wbc[0:4, i * STATE:(i + 1) * STATE] = taps[:, i, :]
            wbc[4:5, i * STATE:(i + 1) * STATE] = offset[i:i + 1]

    bc_in = bc_ref[...].astype(F32)
    bc = conv(bc_in, prevbc[...], wbc[...])
    prevbc[...] = bc_in[BLOCK - 8:]
    bco_ref[...] = bc
    b_across = bc[:, :STATE].astype(F32).T.astype(BF16)

    dt = softplus(dt_ref[...] + own[:, 1:2])
    log = dt * (jnp.exp(own[:, 0:1]) * (-LOG2E))
    tri = jnp.where(iota((BLOCK, BLOCK), 0) <= iota((BLOCK, BLOCK), 1), 1.0, 0.0).astype(BF16)
    r = sum(dot(piece, tri) for piece in thirds(log))
    rdt_ref[0] = jnp.concatenate([r, dt], 0)
    r_last = r[:, BLOCK - 1:BLOCK]
    rc[...] = rc[...] + r_last
    tail = jnp.exp2(r_last - r) * dt
    decay = jnp.exp2(jnp.broadcast_to(r_last, (SPAN, BLOCK)))
    factors = jnp.concatenate([pair_halves(tail.T), pair_halves(decay.T[:16])], 0)

    for q in range(WIDTH // QUAD):
        cols = slice(q * QUAD, (q + 1) * QUAD)
        x_in = x_ref[:, cols].astype(F32)
        xc = conv(x_in, prevx[:, cols], wx[:, cols])
        prevx[:, cols] = x_in[BLOCK - 8:]
        xc_ref[:, cols] = xc
        factor = spread_heads(factors, spread[:, cols])
        carried = (xc.astype(F32) * factor[:BLOCK]).astype(BF16)
        car_ref[:, cols] = carried
        fresh = dot(b_across, carried)
        state[:, cols] = state[:, cols] * factor[BLOCK:BLOCK + 1] + fresh

    @pl.when(block_at == pl.num_programs(0) - 1)
    def _():
        decays = spread_heads(pair_halves(jnp.exp2(rc[...]).T[:16]), spread[...])
        for c in range(RANKS):
            cols = slice(c * 128, (c + 1) * 128)
            send_ref[c, 0:STATE, :] = state[:, cols]
            send_ref[c, STATE:, :] = decays[0:8, cols]


def inner_kernel(at_ref, xc_ref, bc_ref, rdt_ref, alog_ref, bias_ref, skip_ref, yl_ref, skip):
    @pl.when(pl.program_id(0) == 0)
    def _():
        spread = jnp.where(
            iota((SPAN, WIDTH), 1) // HEAD == iota((SPAN, WIDTH), 0), 1.0, 0.0).astype(BF16)
        own = own_heads(at_ref[0], alog_ref, bias_ref, skip_ref)
        skip[...] = sum(dot(p, spread, ((0,), (0,))) for p in thirds(own))

    b_now = bc_ref[:, :STATE]
    c_now = bc_ref[:, STATE:]
    scores = dot(c_now, b_now, ((1,), (1,)))
    scores = jnp.where(iota((BLOCK, BLOCK), 1) <= iota((BLOCK, BLOCK), 0), scores, 0.0)
    along = rdt_ref[0]
    r = along.T
    left = iota((BLOCK, 128), 1) < HEAD

    for q in range(WIDTH // QUAD):
        cols = slice(q * QUAD, (q + 1) * QUAD)
        xq = xc_ref[:, cols]
        parts = []
        for pair in range(2):
            weights = []
            for h in (4 * q + 2 * pair, 4 * q + 2 * pair + 1):
                gap = jnp.minimum(r[:, h:h + 1] - along[h:h + 1, :], 0.0)
                weight = jnp.exp2(gap) * (scores * along[SPAN + h:SPAN + h + 1, :])
                weights.append(weight.astype(BF16))
            xp = xq[:, pair * 128:(pair + 1) * 128]
            none = jnp.zeros_like(xp)
            rhs = jnp.concatenate([jnp.where(left, xp, none), jnp.where(left, none, xp)], 0)
            parts.append(dot(jnp.concatenate(weights, 1), rhs))
        out = jnp.concatenate(parts, 1) + skip[2:3, cols] * xq.astype(F32)
        yl_ref[:, cols] = out.astype(BF16)


def chosen_rows(traj):
    hit = jnp.broadcast_to(jnp.where(traj == 0, 1.0, 0.0), (8, ROWS))
    ahead = jnp.where(iota((ROWS, ROWS), 0) < iota((ROWS, ROWS), 1), 1.0, 0.0).astype(BF16)
    rank = dot(hit.astype(BF16), ahead)
    return jnp.where((rank == iota((8, ROWS), 0).astype(F32)) & (hit > 0.5), 1.0, 0.0)


def last_kernel(got_ref, prior_ref, reads_ref, first_ref, state):
    @pl.when(pl.program_id(0) == 0)
    def _():
        state[...] = prior_ref[...].astype(F32).T

    held = state[...]
    for c in range(got_ref.shape[0]):
        held = held * got_ref[c, STATE:STATE + 1, :] + got_ref[c, 0:STATE, :]
    state[...] = held

    @pl.when(pl.program_id(0) == pl.num_programs(0) - 1)
    def _():
        hi, lo = halves(held)
        reads = reads_ref[...].astype(BF16)
        first_ref[...] = dot(reads, hi) + dot(reads, lo)


def scan_kernel(got_ref, prior_ref, first_ref, enter_ref, state):
    @pl.when(pl.program_id(0) == 0)
    def _():
        state[...] = prior_ref[...].astype(F32).T

    held = state[...]
    for c in range(got_ref.shape[0]):
        enter_ref[c] = held
        held = held * got_ref[c, STATE:STATE + 1, :] + got_ref[c, 0:STATE, :]
    state[...] = held


def out_kernel(at_ref, yl_ref, car_ref, bc_ref, rdt_ref, in_ref, z_ref, gain_ref, out_ref,
               spread, state, mixed):
    @pl.when(pl.program_id(0) == 0)
    def _():
        fill_expander(spread)
        for c in range(RANKS):
            state[:, c * 128:(c + 1) * 128] = in_ref[c]

    b_across = bc_ref[:, :STATE].astype(F32).T.astype(BF16)
    c_now = bc_ref[:, STATE:]
    factors = pair_halves(jnp.exp2(rdt_ref[0, 0:SPAN, :]).T)
    total = jnp.zeros((BLOCK, 128), F32)
    for q in range(WIDTH // QUAD):
        cols = slice(q * QUAD, (q + 1) * QUAD)
        factor = spread_heads(factors, spread[:, cols])
        held = state[:, cols]
        y = yl_ref[:, cols].astype(F32) + dot(c_now, held.astype(BF16)) * factor
        fresh = dot(b_across, car_ref[:, cols])
        state[:, cols] = held * factor[BLOCK - 1:BLOCK] + fresh
        m = y * silu(z_ref[:, cols].astype(F32))
        mixed[:, cols] = m
        sq = m * m
        total = total + sq[:, :128] + sq[:, 128:]
    mean = jnp.sum(total, axis=1, keepdims=True) * (1.0 / WIDTH)
    scale = lax.rsqrt(mean + EPSILON)
    for q in range(WIDTH // QUAD):
        cols = slice(q * QUAD, (q + 1) * QUAD)
        out_ref[:, cols] = (mixed[:, cols] * scale * gain_ref[:, cols]).astype(BF16)


def two_heads(at_ref, ref):
    first = at_ref[0]
    lane = iota((1, 128), 1)
    return jnp.where(lane < HEAD, ref[first], ref[first + 1])


def decode_kernel(at_ref, alog_ref, bias_ref, skip_ref, slot_ref, cache_ref, bc_ref, x_ref, dt_ref,
                  traj_ref, y_ref, d_ref, reads_ref, order, held_b, held_c, sorted_c, reads):
    step = pl.program_id(0)

    @pl.when(step == 0)
    def _():
        traj = jnp.broadcast_to(traj_ref[...].astype(F32), (ROWS, ROWS))
        sub, lane = iota((ROWS, ROWS), 0), iota((ROWS, ROWS), 1)
        rank = jnp.sum(jnp.where((traj == traj.T) & (sub < lane), 1.0, 0.0), axis=0, keepdims=True)
        place = traj_ref[...].astype(F32) * 4.0 + rank
        order[...] = jnp.where(sub.astype(F32) == place, 1.0, 0.0).astype(BF16)

    shape = (96, 512)
    out, line = iota(shape, 0), iota(shape, 1)
    group = jnp.where(out < 64, at_ref[1], at_ref[2])
    wanted = (out % 32) * 16 + jnp.where(out < 32, 0, 8) + group
    pick = jnp.where(line == wanted, 1.0, 0.0).astype(BF16)
    prefill_c = []
    for g in range(ROWS // 32):
        got = dot(pick, bc_ref[g * 512:(g + 1) * 512, :]).astype(BF16)
        held_b[step, g * 32:(g + 1) * 32, :] = got[0:32]
        held_c[step, g * 32:(g + 1) * 32, :] = got[32:64]
        prefill_c.append(got[64:96])
    sorted_c[step] = dot(order[...], held_c[step]).astype(BF16)
    chosen = chosen_rows(traj_ref[...]).astype(BF16)
    reads_ref[...] = dot(chosen, jnp.concatenate(prefill_c, 0))

    @pl.when(step == STEPS - 1)
    def _():
        for g in range(ROWS // 16):
            lhs = jnp.concatenate([sorted_c[k, g * 16:(g + 1) * 16, :] for k in range(STEPS)], 0)
            row = iota((16 * STEPS, 128), 0) % 16 // 4
            out = jnp.zeros((16 * STEPS, 128), F32)
            for i in range(4):
                if g == 0 and i == 0:
                    continue
                got = dot(lhs, cache_ref[slot_ref[4 * g + i]], ((1,), (1,)))
                out = jnp.where(row == i, got, out)
            for k in range(STEPS):
                reads[k, g * 16:(g + 1) * 16, :] = out[k * 16:(k + 1) * 16]

        rate = jnp.exp(two_heads(at_ref, alog_ref)) * (-LOG2E)
        bias = two_heads(at_ref, bias_ref)
        skip = two_heads(at_ref, skip_ref)
        upper = iota((128, ROWS), 0) < HEAD
        total = jnp.ones((ROWS, 128), F32)
        pushed = []
        for k in range(STEPS):
            raw = dt_ref[k]
            dt = softplus(jnp.where(upper, raw[0:1, :], raw[1:2, :]).T + bias)
            x_now = x_ref[k].astype(F32)
            decay = jnp.exp2(dt * rate)
            total = total * decay
            pushed = [p * decay for p in pushed] + [dt * x_now]
            hi, lo = halves(reads[k])
            back = dot(order[...], hi, ((0,), (0,))) + dot(order[...], lo, ((0,), (0,)))
            y = total * back + skip * x_now
            c_now = held_c[k].astype(F32)
            for j in range(k + 1):
                met = jnp.sum(held_b[j].astype(F32) * c_now, axis=1, keepdims=True)
                y = y + pushed[j] * met
            y_ref[k] = y
            d_ref[k] = total


def mix_kernel(y_ref, d_ref, first_ref, z_ref, traj_ref, m_ref, sq_ref):
    pick = chosen_rows(traj_ref[...]).astype(BF16)
    ones = jnp.ones((8, 128), BF16)
    sq_ref[...] = jnp.zeros_like(sq_ref)
    for k in range(STEPS):
        hi, lo = halves(first_ref[k * 8:(k + 1) * 8, :])
        read = dot(pick, hi, ((0,), (0,))) + dot(pick, lo, ((0,), (0,)))
        m = (y_ref[k] + d_ref[k] * read) * silu(z_ref[k].astype(F32))
        m_ref[k] = m
        hi, lo = halves(m * m)
        sums = dot(ones, hi, ((1,), (1,))) + dot(ones, lo, ((1,), (1,)))
        sq_ref[k:k + 1, :] = sums[0:1]


def norm_kernel(at_ref, m_ref, sq_ref, gain_ref, out_ref):
    for k in range(STEPS):
        scale = lax.rsqrt(sq_ref[k:k + 1, :] * (1.0 / WIDTH) + EPSILON)
        scale = jnp.broadcast_to(scale, (ROWS, ROWS)).T
        out_ref[k] = (m_ref[k] * scale * gain_ref[...]).astype(BF16)


def full(shape):
    return pl.BlockSpec(shape, lambda *_: (0,) * len(shape))


def params(mib=60):
    return pltpu.CompilerParams(vmem_limit_bytes=mib * 2**20)


def cost(flops, nbytes):
    return pl.CostEstimate(flops=flops, bytes_accessed=nbytes, transcendentals=0)


def local(x_tokens, bc_tokens, z_tokens, dt_tokens, conv_x, conv_bc, bias_x, bias_bc, a_log, dt_bias,
          d_skip, norm_gain, state_cache, traj_slot, row_traj, x_decode, bc_decode, z_decode,
          dt_decode):
    ctx_at = lax.axis_index("ctx").astype(jnp.int32)
    head_at = lax.axis_index("head").astype(jnp.int32)
    flat = ctx_at * 8 + head_at
    tokens = x_tokens.shape[0]
    blocks = tokens // BLOCK
    vmem = pl.BlockSpec(memory_space=pltpu.VMEM)
    smem = pl.BlockSpec(memory_space=pltpu.SMEM)

    bc_flat = bc_tokens.reshape(tokens, 2 * STATE)
    edge = jnp.concatenate(
        [x_tokens[tokens - 3:], bc_tokens[tokens - 3:].reshape(3, 2 * STATE)], 1)
    edge = lax.ppermute(edge, "ctx", [(i, i + 1) for i in range(RANKS - 1)])
    owners = [(16 * g + c, 8 * c + g) for c in range(RANKS) for g in range(8)]
    prior = state_cache[traj_slot[0]].reshape(128, STATE)
    prior = lax.ppermute(prior, ("ctx", "head"), owners)

    traj = row_traj.reshape(1, ROWS)
    here = jnp.reshape(head_at, (1,))
    per_head = [v.reshape(1, -1) for v in (a_log, dt_bias, d_skip)]
    head_specs = [full((1, a_log.shape[0]))] * 3

    rows = lambda width, at=0: pl.BlockSpec((BLOCK, width), lambda b, *_: (b, at))
    times = pl.BlockSpec((1, 2 * SPAN, BLOCK), lambda b, *_: (b, 0, 0))
    xc, car, bc, rdt, send = pl.pallas_call(
        prep_kernel,
        grid_spec=pltpu.PrefetchScalarGridSpec(
            num_scalar_prefetch=1,
            grid=(blocks,),
            in_specs=[rows(WIDTH), rows(2 * STATE), full((3, WIDTH + 2 * STATE)),
                      pl.BlockSpec((SPAN, BLOCK), lambda b, *_: (0, b)), *head_specs,
                      full((4, WIDTH)), full((WIDTH // 128, 128)), full((4, 2, STATE)),
                      full((2, STATE))],
            out_specs=[rows(WIDTH), rows(WIDTH), rows(2 * STATE), times,
                       full((RANKS, STATE + 8, 128))],
            scratch_shapes=[pltpu.VMEM((8, WIDTH), F32), pltpu.VMEM((8, 2 * STATE), F32),
                            pltpu.VMEM((STATE, WIDTH), F32), pltpu.VMEM((SPAN, BLOCK), F32),
                            pltpu.VMEM((2 * SPAN, WIDTH), BF16), pltpu.VMEM((SPAN, 8), F32),
                            pltpu.VMEM((8, WIDTH), F32), pltpu.VMEM((8, 2 * STATE), F32)],
        ),
        out_shape=[
            jax.ShapeDtypeStruct((tokens, WIDTH), BF16),
            jax.ShapeDtypeStruct((tokens, WIDTH), BF16),
            jax.ShapeDtypeStruct((tokens, 2 * STATE), BF16),
            jax.ShapeDtypeStruct((blocks, 2 * SPAN, BLOCK), F32),
            jax.ShapeDtypeStruct((RANKS, STATE + 8, 128), F32),
        ],
        compiler_params=params(),
        cost_estimate=cost(8 * 10**9, 20 * 2**20),
        name="prep",
    )(here, x_tokens, bc_flat, edge, dt_tokens.T, *per_head, conv_x, bias_x.reshape(-1, 128),
      conv_bc.reshape(4, 2, STATE), bias_bc.reshape(2, STATE))

    got = lax.all_to_all(send, "ctx", 0, 0)

    yl = pl.pallas_call(
        inner_kernel,
        grid_spec=pltpu.PrefetchScalarGridSpec(
            num_scalar_prefetch=1,
            grid=(blocks,),
            in_specs=[rows(WIDTH), rows(2 * STATE), times, *head_specs],
            out_specs=rows(WIDTH),
            scratch_shapes=[pltpu.VMEM((8, WIDTH), F32)],
        ),
        out_shape=jax.ShapeDtypeStruct((tokens, WIDTH), BF16),
        compiler_params=params(),
        cost_estimate=cost(8 * 10**9, 20 * 2**20),
        name="inner",
    )(here, xc, bc, rdt, *per_head)

    got, yl = lax.optimization_barrier((got, yl))

    lines = ROWS * 16
    at = jnp.stack([flat * 2, ctx_at // 2, head_at])
    whole = full((STEPS, ROWS, 128))
    y_dec, d_dec, reads = pl.pallas_call(
        decode_kernel,
        grid_spec=pltpu.PrefetchScalarGridSpec(
            num_scalar_prefetch=1,
            grid=(STEPS,),
            in_specs=[smem] * 4 + [full(state_cache.reshape(-1, 128, STATE).shape),
                                   pl.BlockSpec((lines, STATE), lambda k, *_: (k, 0)),
                                   whole, full((STEPS, 2, ROWS)), full((1, ROWS))],
            out_specs=[whole, whole, pl.BlockSpec((8, STATE), lambda k, *_: (k, 0))],
            scratch_shapes=[pltpu.VMEM((ROWS, ROWS), BF16)]
            + [pltpu.VMEM((STEPS, ROWS, STATE), BF16)] * 3
            + [pltpu.VMEM((STEPS, ROWS, 128), F32)],
        ),
        out_shape=[jax.ShapeDtypeStruct((STEPS, ROWS, 128), F32)] * 2
        + [jax.ShapeDtypeStruct((8 * STEPS, STATE), F32)],
        compiler_params=params(),
        cost_estimate=cost(2 * 10**9, 6 * 2**20),
        name="decode",
    )(at, a_log, dt_bias, d_skip, traj_slot, state_cache.reshape(-1, 128, STATE),
      bc_decode.reshape(STEPS * lines, STATE), x_decode, jnp.swapaxes(dt_decode, 1, 2), traj)

    some = RANKS // 4
    got_spec = pl.BlockSpec((some, STATE + 8, 128), lambda i: (i, 0, 0))
    first = pl.pallas_call(
        last_kernel,
        grid=(4,),
        in_specs=[got_spec, full((128, STATE)), full((8 * STEPS, STATE))],
        out_specs=full((8 * STEPS, 128)),
        out_shape=jax.ShapeDtypeStruct((8 * STEPS, 128), F32),
        scratch_shapes=[pltpu.VMEM((STATE, 128), F32)],
        compiler_params=params(),
        cost_estimate=cost(10**8, 2 * 2**20),
        name="last",
    )(got, prior, reads)
    enter = pl.pallas_call(
        scan_kernel,
        grid=(4,),
        in_specs=[got_spec, full((128, STATE)), full((8 * STEPS, 128))],
        out_specs=pl.BlockSpec((some, STATE, 128), lambda i: (i, 0, 0)),
        out_shape=jax.ShapeDtypeStruct((RANKS, STATE, 128), F32),
        scratch_shapes=[pltpu.VMEM((STATE, 128), F32)],
        compiler_params=params(),
        cost_estimate=cost(10**8, 4 * 2**20),
        name="scan",
    )(got, prior, first)

    first = lax.ppermute(first, ("ctx", "head"), [(b, a) for a, b in owners])
    enter = lax.all_to_all(enter, "ctx", 0, 0)

    mixed, squares = pl.pallas_call(
        mix_kernel,
        in_specs=[vmem] * 5,
        out_specs=[vmem] * 2,
        out_shape=[jax.ShapeDtypeStruct((STEPS, ROWS, 128), F32),
                   jax.ShapeDtypeStruct((8, ROWS), F32)],
        compiler_params=params(),
        cost_estimate=cost(10**8, 2**20),
        name="mix",
    )(y_dec, d_dec, first, z_decode, traj)

    for away in ((1, 2, 3), (4, 8, 12)):
        squares = squares + sum(
            lax.ppermute(squares, ("ctx", "head"), [(i, i ^ d) for i in range(128)]) for d in away)

    enter, squares = lax.optimization_barrier((enter, squares))
    prefill_out = pl.pallas_call(
        out_kernel,
        grid_spec=pltpu.PrefetchScalarGridSpec(
            num_scalar_prefetch=1,
            grid=(blocks,),
            in_specs=[rows(WIDTH), rows(WIDTH), rows(2 * STATE), times, full((RANKS, STATE, 128)),
                      rows(WIDTH), pl.BlockSpec((1, WIDTH), lambda b, at: (0, at[0]))],
            out_specs=rows(WIDTH),
            scratch_shapes=[pltpu.VMEM((2 * SPAN, WIDTH), BF16), pltpu.VMEM((STATE, WIDTH), F32),
                            pltpu.VMEM((BLOCK, WIDTH), F32)],
        ),
        out_shape=jax.ShapeDtypeStruct((tokens, WIDTH), BF16),
        compiler_params=params(),
        cost_estimate=cost(4 * 10**9, 16 * 2**20),
        name="gate",
    )(here, yl, car, bc, rdt, enter, z_tokens, norm_gain.reshape(1, -1))

    decode_out = pl.pallas_call(
        norm_kernel,
        grid_spec=pltpu.PrefetchScalarGridSpec(
            num_scalar_prefetch=1,
            grid=(1,),
            in_specs=[full((STEPS, ROWS, 128)), full((8, ROWS)),
                      pl.BlockSpec((1, 128), lambda b, at: (0, at[0]))],
            out_specs=full((STEPS, ROWS, 128)),
        ),
        out_shape=jax.ShapeDtypeStruct((STEPS, ROWS, 128), BF16),
        compiler_params=params(),
        cost_estimate=cost(10**7, 2**19),
        name="norm",
    )(jnp.reshape(flat, (1,)), mixed, squares, norm_gain.reshape(1, -1))
    return (prefill_out, decode_out)


def solution(mesh):
    in_specs = (
        P("ctx", "head"),
        P("ctx", None, "head", None),
        P("ctx", "head"),
        P("ctx", "head"),
        P(None, "head"),
        P(None, None, "head", None),
        P("head"),
        P(None, "head", None),
        P(),
        P(),
        P(),
        P(),
        P(None, ("ctx", "head"), None, None),
        P(),
        P(),
        P(None, None, ("ctx", "head")),
        P(),
        P(None, None, ("ctx", "head")),
        P(None, None, ("ctx", "head")),
    )
    out_specs = (P("ctx", "head"), P(None, None, ("ctx", "head")))
    return jax.shard_map(local, mesh=mesh, in_specs=in_specs, out_specs=out_specs, check_vma=False)
```

```python
import jax
import jax.numpy as jnp
from jax import lax
from jax.experimental import pallas as pl
from jax.experimental.pallas import tpu as pltpu
from jax.sharding import PartitionSpec as P

BLOCK = 128
HEAD = 64
STATE = 256
HEADS = 256
SPAN = 32
WIDTH = SPAN * HEAD
RANKS = 16
ROWS = 128
STEPS = 4
SUBS = 2
QUAD = 256
EPSILON = 1e-05
LOG2E = 1.4426950408889634
F32 = jnp.float32
BF16 = jnp.bfloat16


def dot(a, b, dims=((1,), (0,))):
    return lax.dot_general(a, b, (dims, ((), ())), preferred_element_type=F32)


def halves(v):
    hi = v.astype(BF16)
    return hi, (v - hi.astype(F32)).astype(BF16)


def thirds(v):
    hi, mid = halves(v)
    return hi, mid, (v - hi.astype(F32) - mid.astype(F32)).astype(BF16)


def softplus(v):
    return jnp.maximum(v, 0.0) + jnp.log1p(jnp.exp(-jnp.abs(v)))


def silu(v):
    h = 0.5 * v
    return h + h * jnp.tanh(h)


def iota(shape, dim):
    return lax.broadcasted_iota(jnp.int32, shape, dim)


def fill_expander(ref):
    shape = (2 * SPAN, WIDTH)
    ref[...] = jnp.where(iota(shape, 1) // HEAD == iota(shape, 0) % SPAN, 1.0, 0.0).astype(BF16)


def conv(block, before, taps):
    joined = jnp.concatenate([before, block], 0)
    h = taps[4:5] + taps[0:1] * pltpu.roll(joined, 3, 0)[8:]
    h = h + taps[1:2] * pltpu.roll(joined, 2, 0)[8:]
    h = h + taps[2:3] * pltpu.roll(joined, 1, 0)[8:]
    h = h + taps[3:4] * block
    return (h + h * jnp.tanh(h)).astype(BF16)


def own_heads(head_at, alog_ref, bias_ref, skip_ref):
    rows = jnp.concatenate([alog_ref[...], bias_ref[...]] + [skip_ref[...]] * 6, 0)
    shape = (SPAN, rows.shape[1])
    mine = jnp.where(iota(shape, 1) == iota(shape, 0) + head_at * SPAN, 1.0, 0.0).astype(BF16)
    return sum(dot(mine, piece, ((1,), (1,))) for piece in thirds(rows))


def spread_heads(rows, spread):
    return dot(rows, spread)


def pair_halves(rows):
    return jnp.concatenate(halves(rows), 1)


def prep_kernel(at_ref, x_ref, bc_ref, edge_ref, dt_ref, alog_ref, bias_ref, skip_ref, cw_ref, cb_ref,
                bw_ref, bb_ref, xc_ref, car_ref, bco_ref, bt_ref, rdt_ref, er_ref, send_ref,
                prevx, state, spread, wx, wbc, factors, decays):
    step = pl.program_id(0)
    blocks = rdt_ref.shape[0]

    @pl.when(step == 0)
    def _():
        fill_expander(spread)
        own = own_heads(at_ref[0], alog_ref, bias_ref, skip_ref)
        state[...] = jnp.zeros_like(state)
        wx[0:4, :] = cw_ref[...].astype(F32) * 0.5
        offset = cb_ref[...].astype(F32) * 0.5
        for i in range(WIDTH // 128):
            wx[4:5, i * 128:(i + 1) * 128] = offset[i:i + 1]
        taps = bw_ref[...].astype(F32) * 0.5
        offset = bb_ref[...].astype(F32) * 0.5
        for i in range(2):
            wbc[0:4, i * STATE:(i + 1) * STATE] = taps[:, i, :]
            wbc[4:5, i * STATE:(i + 1) * STATE] = offset[i:i + 1]
        edge = edge_ref[...].astype(F32)
        prevx[...] = jnp.zeros_like(prevx)
        prevx[5:8, :] = edge[:, :WIDTH]
        before = jnp.concatenate([jnp.zeros((5, 2 * STATE), F32), edge[:, WIDTH:]], 0)

        dt = softplus(dt_ref[...] + own[:, 1:2])
        log = dt * (jnp.exp(own[:, 0:1]) * (-LOG2E))
        spans = [slice(b * BLOCK, (b + 1) * BLOCK) for b in range(blocks)]
        dt = jnp.concatenate([dt[:, span] for span in spans], 0)
        log = jnp.concatenate([log[:, span] for span in spans], 0)
        tri = jnp.where(iota((BLOCK, BLOCK), 0) <= iota((BLOCK, BLOCK), 1), 1.0, 0.0).astype(BF16)
        r = sum(dot(piece, tri) for piece in thirds(log))
        r_last = r[:, BLOCK - 1:BLOCK]
        tail = jnp.exp2(r_last - r) * dt
        er = jnp.exp2(r)
        wide = jnp.broadcast_to(r_last, r.shape)
        decay = jnp.exp2(wide)
        whole = jnp.zeros((SPAN, BLOCK), F32)
        for b in range(blocks):
            heads = slice(b * SPAN, (b + 1) * SPAN)
            rdt_ref[b] = jnp.concatenate([r[heads], dt[heads]], 0)
            er_ref[b] = pair_halves(er[heads].T)
            factors[b, 0:BLOCK, :] = pair_halves(tail[heads].T)
            factors[b, BLOCK:, :] = pair_halves(decay[heads].T[:16])
            whole = whole + wide[heads]
        decays[...] = pair_halves(jnp.exp2(whole).T[:16])
        for b in range(blocks):
            bc_in = bc_ref[spans[b], :].astype(F32)
            bc = conv(bc_in, before, wbc[...])
            before = bc_in[BLOCK - 8:]
            bco_ref[spans[b], :] = bc
            bt_ref[b] = bc[:, :STATE].astype(F32).T.astype(BF16)

    for sub in range(x_ref.shape[0] // BLOCK):
        block_at = step * (x_ref.shape[0] // BLOCK) + sub
        span = slice(sub * BLOCK, (sub + 1) * BLOCK)
        b_across = bt_ref[block_at]
        lhs = factors[block_at]
        for q in range(WIDTH // QUAD):
            cols = slice(q * QUAD, (q + 1) * QUAD)
            x_in = x_ref[span, cols].astype(F32)
            xc = conv(x_in, prevx[:, cols], wx[:, cols])
            prevx[:, cols] = x_in[BLOCK - 8:]
            xc_ref[span, cols] = xc
            factor = spread_heads(lhs, spread[:, cols])
            carried = (xc.astype(F32) * factor[:BLOCK]).astype(BF16)
            car_ref[span, cols] = carried
            fresh = dot(b_across, carried)
            state[:, cols] = state[:, cols] * factor[BLOCK:BLOCK + 1] + fresh

    @pl.when(step == pl.num_programs(0) - 1)
    def _():
        rows = spread_heads(decays[...], spread[...])
        for c in range(RANKS):
            cols = slice(c * 128, (c + 1) * 128)
            send_ref[c, 0:STATE, :] = state[:, cols]
            send_ref[c, STATE:, :] = rows[0:8, cols]


def inner_kernel(at_ref, xc_ref, bc_ref, rdt_ref, alog_ref, bias_ref, skip_ref, yl_ref, skip):
    @pl.when(pl.program_id(0) == 0)
    def _():
        spread = jnp.where(
            iota((SPAN, WIDTH), 1) // HEAD == iota((SPAN, WIDTH), 0), 1.0, 0.0).astype(BF16)
        own = own_heads(at_ref[0], alog_ref, bias_ref, skip_ref)
        skip[...] = sum(dot(p, spread, ((0,), (0,))) for p in thirds(own))

    b_now = bc_ref[:, :STATE]
    c_now = bc_ref[:, STATE:]
    scores = dot(c_now, b_now, ((1,), (1,)))
    scores = jnp.where(iota((BLOCK, BLOCK), 1) <= iota((BLOCK, BLOCK), 0), scores, 0.0)
    along = rdt_ref[0]
    r = along.T
    left = iota((BLOCK, 128), 1) < HEAD

    for q in range(WIDTH // QUAD):
        cols = slice(q * QUAD, (q + 1) * QUAD)
        xq = xc_ref[:, cols]
        parts = []
        for pair in range(2):
            weights = []
            for h in (4 * q + 2 * pair, 4 * q + 2 * pair + 1):
                gap = jnp.minimum(r[:, h:h + 1] - along[h:h + 1, :], 0.0)
                weight = jnp.exp2(gap) * (scores * along[SPAN + h:SPAN + h + 1, :])
                weights.append(weight.astype(BF16))
            xp = xq[:, pair * 128:(pair + 1) * 128]
            none = jnp.zeros_like(xp)
            rhs = jnp.concatenate([jnp.where(left, xp, none), jnp.where(left, none, xp)], 0)
            parts.append(dot(jnp.concatenate(weights, 1), rhs))
        out = jnp.concatenate(parts, 1) + skip[2:3, cols] * xq.astype(F32)
        yl_ref[:, cols] = out.astype(BF16)


def chosen_rows(traj):
    hit = jnp.broadcast_to(jnp.where(traj == 0, 1.0, 0.0), (8, ROWS))
    ahead = jnp.where(iota((ROWS, ROWS), 0) < iota((ROWS, ROWS), 1), 1.0, 0.0).astype(BF16)
    rank = dot(hit.astype(BF16), ahead)
    return jnp.where((rank == iota((8, ROWS), 0).astype(F32)) & (hit > 0.5), 1.0, 0.0)


def scan_kernel(got_ref, prior_ref, reads_ref, rows_ref, enter_ref, mixed_ref):
    held = prior_ref[...].astype(F32).T
    for c in range(RANKS):
        enter_ref[c, 0:STATE, :] = held
        held = held * got_ref[c, STATE:STATE + 1, :] + got_ref[c, 0:STATE, :]
    hi, lo = halves(held)
    reads = reads_ref[...].astype(BF16)
    count = 8 * STEPS
    y = rows_ref[0:count] + rows_ref[count:2 * count] * (dot(reads, hi) + dot(reads, lo))
    m = y * rows_ref[2 * count:]
    mixed_ref[...] = m
    sums = row_sums(jnp.concatenate([m * m, jnp.zeros((128 - count, 128), F32)], 0))
    for c in range(RANKS):
        enter_ref[c, STATE:, :] = sums


def row_sums(v):
    ones = jnp.ones((8, v.shape[1]), BF16)
    hi, lo = halves(v)
    return dot(ones, hi, ((1,), (1,))) + dot(ones, lo, ((1,), (1,)))


def scales(sums):
    scale = lax.rsqrt(sums * (1.0 / WIDTH) + EPSILON)
    return jnp.broadcast_to(scale, (128, 128)).T


def rows_kernel(at_ref, sums_ref, mixed_ref, gain_ref, rows_ref):
    total = sums_ref[0]
    for c in range(1, RANKS):
        total = total + sums_ref[c]
    scale = scales(total[0:1])[:8 * STEPS]
    rows_ref[...] = (mixed_ref[...] * scale * gain_ref[...]).astype(BF16)


def out_kernel(at_ref, yl_ref, car_ref, c_ref, bt_ref, er_ref, in_ref, z_ref, gain_ref, out_ref,
               spread, state, mixed):
    @pl.when(pl.program_id(0) == 0)
    def _():
        fill_expander(spread)
        for c in range(RANKS):
            state[:, c * 128:(c + 1) * 128] = in_ref[c, 0:STATE, :]

    subs = yl_ref.shape[0] // BLOCK
    for sub in range(subs):
        span = slice(sub * BLOCK, (sub + 1) * BLOCK)
        b_across = bt_ref[sub]
        c_now = c_ref[span, :]
        factors = er_ref[sub]
        total = jnp.zeros((BLOCK, 128), F32)
        for q in range(WIDTH // QUAD):
            cols = slice(q * QUAD, (q + 1) * QUAD)
            factor = spread_heads(factors, spread[:, cols])
            held = state[:, cols]
            y = yl_ref[span, cols].astype(F32) + dot(c_now, held.astype(BF16)) * factor
            fresh = dot(b_across, car_ref[span, cols])
            state[:, cols] = held * factor[BLOCK - 1:BLOCK] + fresh
            m = y * silu(z_ref[span, cols].astype(F32))
            mixed[span, cols] = m
            sq = m * m
            total = total + sq[:, :128] + sq[:, 128:]
        mean = jnp.sum(total, axis=1, keepdims=True) * (1.0 / WIDTH)
        scale = lax.rsqrt(mean + EPSILON)
        for q in range(WIDTH // QUAD):
            cols = slice(q * QUAD, (q + 1) * QUAD)
            out_ref[span, cols] = (mixed[span, cols] * scale * gain_ref[:, cols]).astype(BF16)


def two_heads(at_ref, ref):
    first = at_ref[0]
    lane = iota((1, 128), 1)
    return jnp.where(lane < HEAD, ref[first], ref[first + 1])


def decode_kernel(at_ref, alog_ref, bias_ref, skip_ref, slot_ref, cache_ref, bc_ref, x_ref, dt_ref,
                  traj_ref, z_ref, m_ref, sq_ref, rows_ref, reads_ref,
                  order, held_b, held_c, sorted_c, reads):
    step = pl.program_id(0)

    @pl.when(step == 0)
    def _():
        traj = jnp.broadcast_to(traj_ref[...].astype(F32), (ROWS, ROWS))
        sub, lane = iota((ROWS, ROWS), 0), iota((ROWS, ROWS), 1)
        rank = jnp.sum(jnp.where((traj == traj.T) & (sub < lane), 1.0, 0.0), axis=0, keepdims=True)
        place = traj_ref[...].astype(F32) * 4.0 + rank
        order[...] = jnp.where(sub.astype(F32) == place, 1.0, 0.0).astype(BF16)

    shape = (96, 512)
    out, line = iota(shape, 0), iota(shape, 1)
    group = jnp.where(out < 64, at_ref[1], at_ref[2])
    wanted = (out % 32) * 16 + jnp.where(out < 32, 0, 8) + group
    pick = jnp.where(line == wanted, 1.0, 0.0).astype(BF16)
    prefill_c = []
    for g in range(ROWS // 32):
        got = dot(pick, bc_ref[g * 512:(g + 1) * 512, :]).astype(BF16)
        held_b[step, g * 32:(g + 1) * 32, :] = got[0:32]
        held_c[step, g * 32:(g + 1) * 32, :] = got[32:64]
        prefill_c.append(got[64:96])
    sorted_c[step] = dot(order[...], held_c[step]).astype(BF16)
    chosen = chosen_rows(traj_ref[...]).astype(BF16)
    reads_ref[...] = dot(chosen, jnp.concatenate(prefill_c, 0))

    @pl.when(step == STEPS - 1)
    def _():
        for g in range(ROWS // 16):
            lhs = jnp.concatenate([sorted_c[k, g * 16:(g + 1) * 16, :] for k in range(STEPS)], 0)
            row = iota((16 * STEPS, 128), 0) % 16 // 4
            out = jnp.zeros((16 * STEPS, 128), F32)
            for i in range(4):
                if g == 0 and i == 0:
                    continue
                got = dot(lhs, cache_ref[slot_ref[4 * g + i]], ((1,), (1,)))
                out = jnp.where(row == i, got, out)
            for k in range(STEPS):
                reads[k, g * 16:(g + 1) * 16, :] = out[k * 16:(k + 1) * 16]

        rate = jnp.exp(two_heads(at_ref, alog_ref)) * (-LOG2E)
        bias = two_heads(at_ref, bias_ref)
        skip = two_heads(at_ref, skip_ref)
        upper = iota((128, ROWS), 0) < HEAD
        sq_ref[...] = jnp.zeros_like(sq_ref)
        total = jnp.ones((ROWS, 128), F32)
        pushed = []
        for k in range(STEPS):
            raw = dt_ref[k]
            dt = softplus(jnp.where(upper, raw[0:1, :], raw[1:2, :]).T + bias)
            x_now = x_ref[k].astype(F32)
            decay = jnp.exp2(dt * rate)
            total = total * decay
            pushed = [p * decay for p in pushed] + [dt * x_now]
            hi, lo = halves(reads[k])
            back = dot(order[...], hi, ((0,), (0,))) + dot(order[...], lo, ((0,), (0,)))
            y = total * back + skip * x_now
            c_now = held_c[k].astype(F32)
            for j in range(k + 1):
                met = jnp.sum(held_b[j].astype(F32) * c_now, axis=1, keepdims=True)
                y = y + pushed[j] * met
            gate = silu(z_ref[k].astype(F32))
            m = y * gate
            m_ref[k] = m
            sq_ref[k:k + 1, :] = row_sums(m * m)[0:1]
            for i, part in enumerate((y, total, gate)):
                hi, lo = halves(part)
                at = 8 * (STEPS * i + k)
                rows_ref[at:at + 8, :] = dot(chosen, hi) + dot(chosen, lo)


def norm_kernel(at_ref, m_ref, sq_ref, rows_ref, traj_ref, gain_ref, out_ref):
    chosen = chosen_rows(traj_ref[...]).astype(BF16)
    first = dot(chosen, jnp.ones((8, 128), BF16), ((0,), (0,))) > 0.5
    for k in range(STEPS):
        out = m_ref[k] * scales(sq_ref[k:k + 1, :]) * gain_ref[...]
        rows = dot(chosen, rows_ref[k * 8:(k + 1) * 8, :].astype(BF16), ((0,), (0,)))
        out_ref[k] = jnp.where(first, rows, out).astype(BF16)


def full(shape):
    return pl.BlockSpec(shape, lambda *_: (0,) * len(shape))


def far(x):
    return pltpu.with_memory_space_constraint(x, pltpu.HBM)


def params(mib=24):
    return pltpu.CompilerParams(vmem_limit_bytes=mib * 2**20)


def cost(flops, nbytes):
    return pl.CostEstimate(flops=flops, bytes_accessed=nbytes, transcendentals=0)


def block_rows(width):
    return pl.BlockSpec((BLOCK, width), lambda b, *_: (b, 0))


def block_times():
    return pl.BlockSpec((1, 2 * SPAN, BLOCK), lambda b, *_: (b, 0, 0))


def prep_call(here, x, *rest):
    tokens = x.shape[0]
    blocks = tokens // BLOCK
    rows = pl.BlockSpec((SUBS * BLOCK, WIDTH), lambda b, *_: (b, 0))
    shapes = [((tokens, WIDTH), BF16), ((tokens, WIDTH), BF16), ((tokens, 2 * STATE), BF16),
              ((blocks, STATE, BLOCK), BF16), ((blocks, 2 * SPAN, BLOCK), F32),
              ((blocks, BLOCK, 2 * SPAN), BF16), ((RANKS, STATE + 8, 128), F32)]
    return pl.pallas_call(
        prep_kernel,
        grid_spec=pltpu.PrefetchScalarGridSpec(
            num_scalar_prefetch=1,
            grid=(blocks // SUBS,),
            in_specs=[rows, full((tokens, 2 * STATE)), full((3, WIDTH + 2 * STATE)),
                      full((SPAN, tokens)), *[full((1, HEADS))] * 3, full((4, WIDTH)),
                      full((WIDTH // 128, 128)), full((4, 2, STATE)), full((2, STATE))],
            out_specs=[rows, rows] + [full(shape) for shape, _ in shapes[2:]],
            scratch_shapes=[pltpu.VMEM((8, WIDTH), F32), pltpu.VMEM((STATE, WIDTH), F32),
                            pltpu.VMEM((2 * SPAN, WIDTH), BF16), pltpu.VMEM((8, WIDTH), F32),
                            pltpu.VMEM((8, 2 * STATE), F32),
                            pltpu.VMEM((blocks, BLOCK + 16, 2 * SPAN), BF16),
                            pltpu.VMEM((16, 2 * SPAN), BF16)],
        ),
        out_shape=[pltpu.HBM(shape, dtype) for shape, dtype in shapes],
        compiler_params=params(),
        cost_estimate=cost(8 * 10**9, 20 * 2**20),
        name="prep",
    )(here, x, *rest)


def inner_call(here, xc, *rest):
    tokens = xc.shape[0]
    blocks = tokens // BLOCK
    rows, times, head_specs = block_rows, block_times(), [full((1, HEADS))] * 3
    return pl.pallas_call(
        inner_kernel,
        grid_spec=pltpu.PrefetchScalarGridSpec(
            num_scalar_prefetch=1,
            grid=(blocks,),
            in_specs=[rows(WIDTH), rows(2 * STATE), times, *head_specs],
            out_specs=rows(WIDTH),
            scratch_shapes=[pltpu.VMEM((8, WIDTH), F32)],
        ),
        out_shape=pltpu.HBM((tokens, WIDTH), BF16),
        compiler_params=params(),
        cost_estimate=cost(8 * 10**9, 20 * 2**20),
        name="inner",
    )(here, xc, *rest)


def gate_call(here, yl, *rest):
    tokens = yl.shape[0]
    rows = pl.BlockSpec((SUBS * BLOCK, WIDTH), lambda b, *_: (b, 0))
    return pl.pallas_call(
        out_kernel,
        grid_spec=pltpu.PrefetchScalarGridSpec(
            num_scalar_prefetch=1,
            grid=(tokens // BLOCK // SUBS,),
            in_specs=[rows, rows, pl.BlockSpec((SUBS * BLOCK, STATE), lambda b, *_: (b, 1)),
                      pl.BlockSpec((SUBS, STATE, BLOCK), lambda b, *_: (b, 0, 0)),
                      pl.BlockSpec((SUBS, BLOCK, 2 * SPAN), lambda b, *_: (b, 0, 0)),
                      full((RANKS, STATE + 8, 128)), rows,
                      pl.BlockSpec((1, WIDTH), lambda b, at: (0, at[0]))],
            out_specs=rows,
            scratch_shapes=[pltpu.VMEM((2 * SPAN, WIDTH), BF16), pltpu.VMEM((STATE, WIDTH), F32),
                            pltpu.VMEM((SUBS * BLOCK, WIDTH), F32)],
        ),
        out_shape=jax.ShapeDtypeStruct((tokens, WIDTH), BF16),
        compiler_params=params(),
        cost_estimate=cost(4 * 10**9, 16 * 2**20),
        name="gate",
    )(here, yl, *rest)


def local(x_tokens, bc_tokens, z_tokens, dt_tokens, conv_x, conv_bc, bias_x, bias_bc, a_log, dt_bias,
          d_skip, norm_gain, state_cache, traj_slot, row_traj, x_decode, bc_decode, z_decode,
          dt_decode):
    ctx_at = lax.axis_index("ctx").astype(jnp.int32)
    head_at = lax.axis_index("head").astype(jnp.int32)
    flat = ctx_at * 8 + head_at
    tokens = x_tokens.shape[0]
    vmem = pl.BlockSpec(memory_space=pltpu.VMEM)
    smem = pl.BlockSpec(memory_space=pltpu.SMEM)

    bc_flat = bc_tokens.reshape(tokens, 2 * STATE)
    edge = jnp.concatenate(
        [x_tokens[tokens - 3:], bc_tokens[tokens - 3:].reshape(3, 2 * STATE)], 1)
    edge = lax.ppermute(edge, "ctx", [(i, i + 1) for i in range(RANKS - 1)])
    owners = [(16 * g + c, 8 * c + g) for c in range(RANKS) for g in range(8)]
    prior = state_cache[traj_slot[0]].reshape(128, STATE)
    prior = lax.ppermute(prior, ("ctx", "head"), owners)

    traj = far(row_traj.reshape(1, ROWS))
    here = jnp.reshape(head_at, (1,))
    per_head = [far(v.reshape(1, -1)) for v in (a_log, dt_bias, d_skip)]

    xc, car, bc, bt, rdt, er, send = prep_call(
        here, far(x_tokens), bc_flat, edge, far(dt_tokens.T), *per_head, far(conv_x),
        far(bias_x.reshape(-1, 128)), far(conv_bc.reshape(4, 2, STATE)),
        far(bias_bc.reshape(2, STATE)))

    got = lax.all_to_all(send, "ctx", 0, 0)

    yl = inner_call(here, far(xc), far(bc), far(rdt), *per_head)

    got, yl = lax.optimization_barrier((got, yl))

    lines = ROWS * 16
    at = jnp.stack([flat * 2, ctx_at // 2, head_at])
    whole = full((STEPS, ROWS, 128))
    mixed, squares, rows_dec, reads = pl.pallas_call(
        decode_kernel,
        grid_spec=pltpu.PrefetchScalarGridSpec(
            num_scalar_prefetch=1,
            grid=(STEPS,),
            in_specs=[smem] * 4 + [full(state_cache.reshape(-1, 128, STATE).shape),
                                   pl.BlockSpec((lines, STATE), lambda k, *_: (k, 0)),
                                   whole, full((STEPS, 2, ROWS)), full((1, ROWS)), whole],
            out_specs=[whole, full((8, ROWS)), full((24 * STEPS, 128)),
                       pl.BlockSpec((8, STATE), lambda k, *_: (k, 0))],
            scratch_shapes=[pltpu.VMEM((ROWS, ROWS), BF16)]
            + [pltpu.VMEM((STEPS, ROWS, STATE), BF16)] * 3
            + [pltpu.VMEM((STEPS, ROWS, 128), F32)],
        ),
        out_shape=[jax.ShapeDtypeStruct((STEPS, ROWS, 128), F32),
                   jax.ShapeDtypeStruct((8, ROWS), F32),
                   jax.ShapeDtypeStruct((24 * STEPS, 128), F32),
                   jax.ShapeDtypeStruct((8 * STEPS, STATE), F32)],
        compiler_params=params(),
        cost_estimate=cost(2 * 10**9, 6 * 2**20),
        name="decode",
    )(at, a_log, dt_bias, d_skip, traj_slot, far(state_cache.reshape(-1, 128, STATE)),
      far(bc_decode.reshape(STEPS * lines, STATE)), far(x_decode),
      far(jnp.swapaxes(dt_decode, 1, 2)), traj, far(z_decode))
    rows_dec = lax.ppermute(rows_dec, ("ctx", "head"), owners)

    enter, first = pl.pallas_call(
        scan_kernel,
        in_specs=[vmem] * 4,
        out_specs=[vmem] * 2,
        out_shape=[pltpu.HBM((RANKS, STATE + 8, 128), F32),
                   jax.ShapeDtypeStruct((8 * STEPS, 128), F32)],
        compiler_params=params(16),
        cost_estimate=cost(10**8, 4 * 2**20),
        name="scan",
    )(got, prior, reads, rows_dec)
    enter = lax.all_to_all(enter, "ctx", 0, 0)

    for away in ((1, 2, 3), (4, 8, 12)):
        squares = squares + sum(
            lax.ppermute(squares, ("ctx", "head"), [(i, i ^ d) for i in range(128)]) for d in away)

    enter, squares = lax.optimization_barrier((enter, squares))
    first = pl.pallas_call(
        rows_kernel,
        grid_spec=pltpu.PrefetchScalarGridSpec(
            num_scalar_prefetch=1,
            grid=(1,),
            in_specs=[pl.BlockSpec((RANKS, 8, 128), lambda b, at: (0, STATE // 8, 0)),
                      full((8 * STEPS, 128)), pl.BlockSpec((1, 128), lambda b, at: (0, at[0]))],
            out_specs=full((8 * STEPS, 128)),
        ),
        out_shape=jax.ShapeDtypeStruct((8 * STEPS, 128), BF16),
        compiler_params=params(),
        cost_estimate=cost(10**7, 2**18),
        name="rows",
    )(jnp.reshape(head_at * RANKS + ctx_at, (1,)), enter, first, far(norm_gain.reshape(1, -1)))
    first = lax.ppermute(first, ("ctx", "head"), [(b, a) for a, b in owners])

    prefill_out = gate_call(here, far(yl), far(car), far(bc), far(bt), far(er), enter, far(z_tokens),
                            far(norm_gain.reshape(1, -1)))

    decode_out = pl.pallas_call(
        norm_kernel,
        grid_spec=pltpu.PrefetchScalarGridSpec(
            num_scalar_prefetch=1,
            grid=(1,),
            in_specs=[full((STEPS, ROWS, 128)), full((8, ROWS)), full((8 * STEPS, 128)),
                      full((1, ROWS)), pl.BlockSpec((1, 128), lambda b, at: (0, at[0]))],
            out_specs=full((STEPS, ROWS, 128)),
        ),
        out_shape=jax.ShapeDtypeStruct((STEPS, ROWS, 128), BF16),
        compiler_params=params(),
        cost_estimate=cost(10**7, 2**19),
        name="norm",
    )(jnp.reshape(flat, (1,)), mixed, squares, first, traj,
      far(norm_gain.reshape(1, -1)))
    return (prefill_out, decode_out)


def solution(mesh):
    in_specs = (
        P("ctx", "head"),
        P("ctx", None, "head", None),
        P("ctx", "head"),
        P("ctx", "head"),
        P(None, "head"),
        P(None, None, "head", None),
        P("head"),
        P(None, "head", None),
        P(),
        P(),
        P(),
        P(),
        P(None, ("ctx", "head"), None, None),
        P(),
        P(),
        P(None, None, ("ctx", "head")),
        P(),
        P(None, None, ("ctx", "head")),
        P(None, None, ("ctx", "head")),
    )
    out_specs = (P("ctx", "head"), P(None, None, ("ctx", "head")))
    return jax.shard_map(local, mesh=mesh, in_specs=in_specs, out_specs=out_specs, check_vma=False)
```

```python
import jax
import jax.numpy as jnp
from jax import lax
from jax.experimental import pallas as pl
from jax.experimental.pallas import tpu as pltpu
from jax.sharding import PartitionSpec as P

BLOCK = 128
HEAD = 64
STATE = 256
HEADS = 256
SPAN = 32
WIDTH = SPAN * HEAD
RANKS = 16
ROWS = 128
STEPS = 4
SUBS = 2
QUAD = 256
EPSILON = 1e-05
LOG2E = 1.4426950408889634
F32 = jnp.float32
BF16 = jnp.bfloat16


def dot(a, b, dims=((1,), (0,))):
    return lax.dot_general(a, b, (dims, ((), ())), preferred_element_type=F32)


def halves(v):
    hi = v.astype(BF16)
    return hi, (v - hi.astype(F32)).astype(BF16)


def thirds(v):
    hi, mid = halves(v)
    return hi, mid, (v - hi.astype(F32) - mid.astype(F32)).astype(BF16)


def softplus(v):
    return jnp.maximum(v, 0.0) + jnp.log1p(jnp.exp(-jnp.abs(v)))


def silu(v):
    h = 0.5 * v
    return h + h * jnp.tanh(h)


def iota(shape, dim):
    return lax.broadcasted_iota(jnp.int32, shape, dim)


def fill_expander(ref):
    shape = (2 * SPAN, WIDTH)
    ref[...] = jnp.where(iota(shape, 1) // HEAD == iota(shape, 0) % SPAN, 1.0, 0.0).astype(BF16)


def conv(block, before, taps):
    joined = jnp.concatenate([before, block], 0)
    late = pltpu.roll(joined, 1, 0)
    older = taps[1:2] * joined + taps[0:1] * late
    h = taps[4:5] + pltpu.roll(older, 2, 0)[8:]
    h = h + taps[2:3] * late[8:] + taps[3:4] * block
    return (h + h * jnp.tanh(h)).astype(BF16)


def own_heads(head_at, alog_ref, bias_ref, skip_ref):
    rows = jnp.concatenate([alog_ref[...], bias_ref[...]] + [skip_ref[...]] * 6, 0)
    shape = (SPAN, rows.shape[1])
    mine = jnp.where(iota(shape, 1) == iota(shape, 0) + head_at * SPAN, 1.0, 0.0).astype(BF16)
    return sum(dot(mine, piece, ((1,), (1,))) for piece in thirds(rows))


def spread_heads(rows, spread):
    return dot(rows, spread)


def over_channels(rows, q):
    left = iota((rows.shape[0], 128), 1) < HEAD
    first = q * QUAD // HEAD
    return jnp.concatenate(
        [jnp.where(left, rows[:, h:h + 1], rows[:, h + 1:h + 2])
         for h in range(first, first + QUAD // HEAD, 2)], 1)


def pair_halves(rows):
    return jnp.concatenate(halves(rows), 1)


def prep_kernel(at_ref, x_ref, bc_ref, edge_ref, dt_ref, alog_ref, bias_ref, skip_ref, cw_ref, cb_ref,
                bw_ref, bb_ref, xc_ref, car_ref, bco_ref, bt_ref, rdt_ref, er_ref, send_ref,
                prevx, state, spread, wx, wbc, factors, decays):
    step = pl.program_id(0)
    blocks = rdt_ref.shape[0]

    @pl.when(step == 0)
    def _():
        fill_expander(spread)
        own = own_heads(at_ref[0], alog_ref, bias_ref, skip_ref)
        state[...] = jnp.zeros_like(state)
        wx[0:4, :] = cw_ref[...].astype(F32) * 0.5
        offset = cb_ref[...].astype(F32) * 0.5
        for i in range(WIDTH // 128):
            wx[4:5, i * 128:(i + 1) * 128] = offset[i:i + 1]
        taps = bw_ref[...].astype(F32) * 0.5
        offset = bb_ref[...].astype(F32) * 0.5
        for i in range(2):
            wbc[0:4, i * STATE:(i + 1) * STATE] = taps[:, i, :]
            wbc[4:5, i * STATE:(i + 1) * STATE] = offset[i:i + 1]
        edge = edge_ref[...].astype(F32)
        prevx[...] = jnp.zeros_like(prevx)
        prevx[5:8, :] = edge[:, :WIDTH]
        before = jnp.concatenate([jnp.zeros((5, 2 * STATE), F32), edge[:, WIDTH:]], 0)

        dt = softplus(dt_ref[...] + own[:, 1:2])
        log = dt * (jnp.exp(own[:, 0:1]) * (-LOG2E))
        spans = [slice(b * BLOCK, (b + 1) * BLOCK) for b in range(blocks)]
        dt = jnp.concatenate([dt[:, span] for span in spans], 0)
        log = jnp.concatenate([log[:, span] for span in spans], 0)
        tri = jnp.where(iota((BLOCK, BLOCK), 0) <= iota((BLOCK, BLOCK), 1), 1.0, 0.0).astype(BF16)
        r = sum(dot(piece, tri) for piece in thirds(log))
        r_last = r[:, BLOCK - 1:BLOCK]
        tail = jnp.exp2(r_last - r) * dt
        er = jnp.exp2(r)
        wide = jnp.broadcast_to(r_last, r.shape)
        decay = jnp.exp2(wide)
        whole = jnp.zeros((SPAN, BLOCK), F32)
        for b in range(blocks):
            heads = slice(b * SPAN, (b + 1) * SPAN)
            rdt_ref[b] = jnp.concatenate([r[heads], dt[heads]], 0)
            er_ref[b] = pair_halves(er[heads].T)
            factors[b] = tail[heads].T
            rows = spread_heads(pair_halves(decay[heads].T[:16]), spread[...])
            decays[b:b + 1, :] = rows[0:1]
            whole = whole + wide[heads]
        rows = spread_heads(pair_halves(jnp.exp2(whole).T[:16]), spread[...])
        decays[blocks:blocks + 8, :] = rows[0:8]
        for b in range(blocks):
            bc_in = bc_ref[spans[b], :].astype(F32)
            bc = conv(bc_in, before, wbc[...])
            before = bc_in[BLOCK - 8:]
            bco_ref[spans[b], :] = bc
            bt_ref[b] = bc[:, :STATE].astype(F32).T.astype(BF16)

    for sub in range(x_ref.shape[0] // BLOCK):
        block_at = step * (x_ref.shape[0] // BLOCK) + sub
        span = slice(sub * BLOCK, (sub + 1) * BLOCK)
        b_across = bt_ref[block_at]
        lhs = factors[block_at]
        for q in range(WIDTH // QUAD):
            cols = slice(q * QUAD, (q + 1) * QUAD)
            x_in = x_ref[span, cols].astype(F32)
            xc = conv(x_in, prevx[:, cols], wx[:, cols])
            prevx[:, cols] = x_in[BLOCK - 8:]
            xc_ref[span, cols] = xc
            carried = (xc.astype(F32) * over_channels(lhs, q)).astype(BF16)
            car_ref[span, cols] = carried
            fresh = dot(b_across, carried)
            state[:, cols] = state[:, cols] * decays[pl.ds(block_at, 1), cols] + fresh

    @pl.when(step == pl.num_programs(0) - 1)
    def _():
        for c in range(RANKS):
            cols = slice(c * 128, (c + 1) * 128)
            send_ref[c, 0:STATE, :] = state[:, cols]
            send_ref[c, STATE:, :] = decays[blocks:blocks + 8, cols]


def inner_kernel(at_ref, xc_ref, bc_ref, rdt_ref, alog_ref, bias_ref, skip_ref, yl_ref, skip):
    @pl.when(pl.program_id(0) == 0)
    def _():
        spread = jnp.where(
            iota((SPAN, WIDTH), 1) // HEAD == iota((SPAN, WIDTH), 0), 1.0, 0.0).astype(BF16)
        own = own_heads(at_ref[0], alog_ref, bias_ref, skip_ref)
        skip[...] = sum(dot(p, spread, ((0,), (0,))) for p in thirds(own))

    b_now = bc_ref[:, :STATE]
    c_now = bc_ref[:, STATE:]
    scores = dot(c_now, b_now, ((1,), (1,)))
    scores = jnp.where(iota((BLOCK, BLOCK), 1) <= iota((BLOCK, BLOCK), 0), scores, 0.0)
    along = rdt_ref[0]
    r = along.T
    left = iota((BLOCK, 128), 1) < HEAD

    for q in range(WIDTH // QUAD):
        cols = slice(q * QUAD, (q + 1) * QUAD)
        xq = xc_ref[:, cols]
        parts = []
        for pair in range(2):
            weights = []
            for h in (4 * q + 2 * pair, 4 * q + 2 * pair + 1):
                gap = jnp.minimum(r[:, h:h + 1] - along[h:h + 1, :], 0.0)
                weight = jnp.exp2(gap) * (scores * along[SPAN + h:SPAN + h + 1, :])
                weights.append(weight.astype(BF16))
            xp = xq[:, pair * 128:(pair + 1) * 128]
            none = jnp.zeros_like(xp)
            rhs = jnp.concatenate([jnp.where(left, xp, none), jnp.where(left, none, xp)], 0)
            parts.append(dot(jnp.concatenate(weights, 1), rhs))
        out = jnp.concatenate(parts, 1) + skip[2:3, cols] * xq.astype(F32)
        yl_ref[:, cols] = out.astype(BF16)


def chosen_rows(traj):
    hit = jnp.broadcast_to(jnp.where(traj == 0, 1.0, 0.0), (8, ROWS))
    ahead = jnp.where(iota((ROWS, ROWS), 0) < iota((ROWS, ROWS), 1), 1.0, 0.0).astype(BF16)
    rank = dot(hit.astype(BF16), ahead)
    return jnp.where((rank == iota((8, ROWS), 0).astype(F32)) & (hit > 0.5), 1.0, 0.0)


def scan_kernel(got_ref, prior_ref, reads_ref, rows_ref, enter_ref, mixed_ref):
    held = prior_ref[...].astype(F32).T
    for c in range(RANKS):
        enter_ref[c, 0:STATE, :] = held
        held = held * got_ref[c, STATE:STATE + 1, :] + got_ref[c, 0:STATE, :]
    hi, lo = halves(held)
    reads = reads_ref[...].astype(BF16)
    count = 8 * STEPS
    y = rows_ref[0:count] + rows_ref[count:2 * count] * (dot(reads, hi) + dot(reads, lo))
    m = y * rows_ref[2 * count:]
    mixed_ref[...] = m
    sums = row_sums(jnp.concatenate([m * m, jnp.zeros((128 - count, 128), F32)], 0))
    for c in range(RANKS):
        enter_ref[c, STATE:, :] = sums


def row_sums(v):
    ones = jnp.ones((8, v.shape[1]), BF16)
    hi, lo = halves(v)
    return dot(ones, hi, ((1,), (1,))) + dot(ones, lo, ((1,), (1,)))


def scales(sums):
    scale = lax.rsqrt(sums * (1.0 / WIDTH) + EPSILON)
    return jnp.broadcast_to(scale, (128, 128)).T


def rows_kernel(at_ref, sums_ref, mixed_ref, gain_ref, rows_ref):
    total = sums_ref[0]
    for c in range(1, RANKS):
        total = total + sums_ref[c]
    scale = scales(total[0:1])[:8 * STEPS]
    rows_ref[...] = (mixed_ref[...] * scale * gain_ref[...]).astype(BF16)


def out_kernel(at_ref, yl_ref, car_ref, c_ref, bt_ref, er_ref, in_ref, z_ref, gain_ref, out_ref,
               spread, state, mixed):
    @pl.when(pl.program_id(0) == 0)
    def _():
        fill_expander(spread)
        for c in range(RANKS):
            state[:, c * 128:(c + 1) * 128] = in_ref[c, 0:STATE, :]

    subs = yl_ref.shape[0] // BLOCK
    scale = None
    for sub in range(subs + 1):
        span = slice(sub * BLOCK, (sub + 1) * BLOCK)
        done = slice((sub - 1) * BLOCK, sub * BLOCK)
        total = jnp.zeros((BLOCK, 128), F32)
        for q in range(WIDTH // QUAD):
            cols = slice(q * QUAD, (q + 1) * QUAD)
            if sub < subs:
                factor = spread_heads(er_ref[sub], spread[:, cols])
                held = state[:, cols]
                y = yl_ref[span, cols].astype(F32) + dot(c_ref[span, :], held.astype(BF16)) * factor
                fresh = dot(bt_ref[sub], car_ref[span, cols])
                state[:, cols] = held * factor[BLOCK - 1:BLOCK] + fresh
                m = y * silu(z_ref[span, cols].astype(F32))
                mixed[span, cols] = m
                sq = m * m
                total = total + sum(sq[:, i:i + 128] for i in range(0, QUAD, 128))
            if sub > 0:
                out_ref[done, cols] = (mixed[done, cols] * scale * gain_ref[:, cols]).astype(BF16)
        mean = jnp.sum(total, axis=1, keepdims=True) * (1.0 / WIDTH)
        scale = lax.rsqrt(mean + EPSILON)


def two_heads(at_ref, ref):
    first = at_ref[0]
    lane = iota((1, 128), 1)
    return jnp.where(lane < HEAD, ref[first], ref[first + 1])


def decode_kernel(at_ref, alog_ref, bias_ref, skip_ref, slot_ref, cache_ref, bc_ref, x_ref, dt_ref,
                  traj_ref, z_ref, m_ref, sq_ref, rows_ref, reads_ref,
                  order, held_b, held_c, sorted_c, reads):
    step = pl.program_id(0)

    @pl.when(step == 0)
    def _():
        traj = jnp.broadcast_to(traj_ref[...].astype(F32), (ROWS, ROWS))
        sub, lane = iota((ROWS, ROWS), 0), iota((ROWS, ROWS), 1)
        rank = jnp.sum(jnp.where((traj == traj.T) & (sub < lane), 1.0, 0.0), axis=0, keepdims=True)
        place = traj_ref[...].astype(F32) * 4.0 + rank
        order[...] = jnp.where(sub.astype(F32) == place, 1.0, 0.0).astype(BF16)

    shape = (96, 512)
    out, line = iota(shape, 0), iota(shape, 1)
    group = jnp.where(out < 64, at_ref[1], at_ref[2])
    wanted = (out % 32) * 16 + jnp.where(out < 32, 0, 8) + group
    pick = jnp.where(line == wanted, 1.0, 0.0).astype(BF16)
    prefill_c = []
    for g in range(ROWS // 32):
        got = dot(pick, bc_ref[g * 512:(g + 1) * 512, :]).astype(BF16)
        held_b[step, g * 32:(g + 1) * 32, :] = got[0:32]
        held_c[step, g * 32:(g + 1) * 32, :] = got[32:64]
        prefill_c.append(got[64:96])
    sorted_c[step] = dot(order[...], held_c[step]).astype(BF16)
    chosen = chosen_rows(traj_ref[...]).astype(BF16)
    reads_ref[...] = dot(chosen, jnp.concatenate(prefill_c, 0))

    @pl.when(step == STEPS - 1)
    def _():
        for g in range(ROWS // 16):
            lhs = jnp.concatenate([sorted_c[k, g * 16:(g + 1) * 16, :] for k in range(STEPS)], 0)
            row = iota((16 * STEPS, 128), 0) % 16 // 4
            out = jnp.zeros((16 * STEPS, 128), F32)
            for i in range(4):
                if g == 0 and i == 0:
                    continue
                got = dot(lhs, cache_ref[slot_ref[4 * g + i]], ((1,), (1,)))
                out = jnp.where(row == i, got, out)
            for k in range(STEPS):
                reads[k, g * 16:(g + 1) * 16, :] = out[k * 16:(k + 1) * 16]

        rate = jnp.exp(two_heads(at_ref, alog_ref)) * (-LOG2E)
        bias = two_heads(at_ref, bias_ref)
        skip = two_heads(at_ref, skip_ref)
        upper = iota((128, ROWS), 0) < HEAD
        sq_ref[...] = jnp.zeros_like(sq_ref)
        total = jnp.ones((ROWS, 128), F32)
        pushed = []
        for k in range(STEPS):
            raw = dt_ref[k]
            dt = softplus(jnp.where(upper, raw[0:1, :], raw[1:2, :]).T + bias)
            x_now = x_ref[k].astype(F32)
            decay = jnp.exp2(dt * rate)
            total = total * decay
            pushed = [p * decay for p in pushed] + [dt * x_now]
            hi, lo = halves(reads[k])
            back = dot(order[...], hi, ((0,), (0,))) + dot(order[...], lo, ((0,), (0,)))
            y = total * back + skip * x_now
            c_now = held_c[k].astype(F32)
            for j in range(k + 1):
                met = jnp.sum(held_b[j].astype(F32) * c_now, axis=1, keepdims=True)
                y = y + pushed[j] * met
            gate = silu(z_ref[k].astype(F32))
            m = y * gate
            m_ref[k] = m
            sq_ref[k:k + 1, :] = row_sums(m * m)[0:1]
            for i, part in enumerate((y, total, gate)):
                hi, lo = halves(part)
                at = 8 * (STEPS * i + k)
                rows_ref[at:at + 8, :] = dot(chosen, hi) + dot(chosen, lo)


def norm_kernel(at_ref, m_ref, sq_ref, rows_ref, traj_ref, gain_ref, out_ref):
    chosen = chosen_rows(traj_ref[...]).astype(BF16)
    first = dot(chosen, jnp.ones((8, 128), BF16), ((0,), (0,))) > 0.5
    for k in range(STEPS):
        out = m_ref[k] * scales(sq_ref[k:k + 1, :]) * gain_ref[...]
        rows = dot(chosen, rows_ref[k * 8:(k + 1) * 8, :].astype(BF16), ((0,), (0,)))
        out_ref[k] = jnp.where(first, rows, out).astype(BF16)


def full(shape):
    return pl.BlockSpec(shape, lambda *_: (0,) * len(shape))


def far(x):
    return pltpu.with_memory_space_constraint(x, pltpu.HBM)


def params(mib=24):
    return pltpu.CompilerParams(vmem_limit_bytes=mib * 2**20)


def cost(flops, nbytes):
    return pl.CostEstimate(flops=flops, bytes_accessed=nbytes, transcendentals=0)


def block_rows(width):
    return pl.BlockSpec((BLOCK, width), lambda b, *_: (b, 0))


def block_times():
    return pl.BlockSpec((1, 2 * SPAN, BLOCK), lambda b, *_: (b, 0, 0))


def prep_call(here, x, *rest):
    tokens = x.shape[0]
    blocks = tokens // BLOCK
    rows = pl.BlockSpec((SUBS * BLOCK, WIDTH), lambda b, *_: (b, 0))
    shapes = [((tokens, WIDTH), BF16), ((tokens, WIDTH), BF16), ((tokens, 2 * STATE), BF16),
              ((blocks, STATE, BLOCK), BF16), ((blocks, 2 * SPAN, BLOCK), F32),
              ((blocks, BLOCK, 2 * SPAN), BF16), ((RANKS, STATE + 8, 128), F32)]
    return pl.pallas_call(
        prep_kernel,
        grid_spec=pltpu.PrefetchScalarGridSpec(
            num_scalar_prefetch=1,
            grid=(blocks // SUBS,),
            in_specs=[rows, full((tokens, 2 * STATE)), full((3, WIDTH + 2 * STATE)),
                      full((SPAN, tokens)), *[full((1, HEADS))] * 3, full((4, WIDTH)),
                      full((WIDTH // 128, 128)), full((4, 2, STATE)), full((2, STATE))],
            out_specs=[rows, rows] + [full(shape) for shape, _ in shapes[2:]],
            scratch_shapes=[pltpu.VMEM((8, WIDTH), F32), pltpu.VMEM((STATE, WIDTH), F32),
                            pltpu.VMEM((2 * SPAN, WIDTH), BF16), pltpu.VMEM((8, WIDTH), F32),
                            pltpu.VMEM((8, 2 * STATE), F32),
                            pltpu.VMEM((blocks, BLOCK, SPAN), F32),
                            pltpu.VMEM((blocks + 8, WIDTH), F32)],
        ),
        out_shape=[pltpu.HBM(shape, dtype) for shape, dtype in shapes],
        compiler_params=params(),
        cost_estimate=cost(8 * 10**9, 20 * 2**20),
        name="prep",
    )(here, x, *rest)


def inner_call(here, xc, *rest):
    tokens = xc.shape[0]
    blocks = tokens // BLOCK
    rows, times, head_specs = block_rows, block_times(), [full((1, HEADS))] * 3
    return pl.pallas_call(
        inner_kernel,
        grid_spec=pltpu.PrefetchScalarGridSpec(
            num_scalar_prefetch=1,
            grid=(blocks,),
            in_specs=[rows(WIDTH), rows(2 * STATE), times, *head_specs],
            out_specs=rows(WIDTH),
            scratch_shapes=[pltpu.VMEM((8, WIDTH), F32)],
        ),
        out_shape=pltpu.HBM((tokens, WIDTH), BF16),
        compiler_params=params(),
        cost_estimate=cost(8 * 10**9, 20 * 2**20),
        name="inner",
    )(here, xc, *rest)


def gate_call(here, yl, *rest):
    tokens = yl.shape[0]
    rows = pl.BlockSpec((SUBS * BLOCK, WIDTH), lambda b, *_: (b, 0))
    return pl.pallas_call(
        out_kernel,
        grid_spec=pltpu.PrefetchScalarGridSpec(
            num_scalar_prefetch=1,
            grid=(tokens // BLOCK // SUBS,),
            in_specs=[rows, rows, pl.BlockSpec((SUBS * BLOCK, STATE), lambda b, *_: (b, 1)),
                      pl.BlockSpec((SUBS, STATE, BLOCK), lambda b, *_: (b, 0, 0)),
                      pl.BlockSpec((SUBS, BLOCK, 2 * SPAN), lambda b, *_: (b, 0, 0)),
                      full((RANKS, STATE + 8, 128)), rows,
                      pl.BlockSpec((1, WIDTH), lambda b, at: (0, at[0]))],
            out_specs=rows,
            scratch_shapes=[pltpu.VMEM((2 * SPAN, WIDTH), BF16), pltpu.VMEM((STATE, WIDTH), F32),
                            pltpu.VMEM((SUBS * BLOCK, WIDTH), F32)],
        ),
        out_shape=jax.ShapeDtypeStruct((tokens, WIDTH), BF16),
        compiler_params=params(),
        cost_estimate=cost(4 * 10**9, 16 * 2**20),
        name="gate",
    )(here, yl, *rest)


def local(x_tokens, bc_tokens, z_tokens, dt_tokens, conv_x, conv_bc, bias_x, bias_bc, a_log, dt_bias,
          d_skip, norm_gain, state_cache, traj_slot, row_traj, x_decode, bc_decode, z_decode,
          dt_decode):
    ctx_at = lax.axis_index("ctx").astype(jnp.int32)
    head_at = lax.axis_index("head").astype(jnp.int32)
    flat = ctx_at * 8 + head_at
    tokens = x_tokens.shape[0]
    vmem = pl.BlockSpec(memory_space=pltpu.VMEM)
    smem = pl.BlockSpec(memory_space=pltpu.SMEM)

    bc_flat = bc_tokens.reshape(tokens, 2 * STATE)
    edge = jnp.concatenate(
        [x_tokens[tokens - 3:], bc_tokens[tokens - 3:].reshape(3, 2 * STATE)], 1)
    edge = lax.ppermute(edge, "ctx", [(i, i + 1) for i in range(RANKS - 1)])
    owners = [(16 * g + c, 8 * c + g) for c in range(RANKS) for g in range(8)]
    prior = state_cache[traj_slot[0]].reshape(128, STATE)
    prior = lax.ppermute(prior, ("ctx", "head"), owners)

    traj = far(row_traj.reshape(1, ROWS))
    here = jnp.reshape(head_at, (1,))
    per_head = [far(v.reshape(1, -1)) for v in (a_log, dt_bias, d_skip)]

    xc, car, bc, bt, rdt, er, send = prep_call(
        here, far(x_tokens), bc_flat, edge, far(dt_tokens.T), *per_head, far(conv_x),
        far(bias_x.reshape(-1, 128)), far(conv_bc.reshape(4, 2, STATE)),
        far(bias_bc.reshape(2, STATE)))

    got = lax.all_to_all(send, "ctx", 0, 0)

    yl = inner_call(here, far(xc), far(bc), far(rdt), *per_head)
    got, yl = lax.optimization_barrier((got, yl))

    lines = ROWS * 16
    at = jnp.stack([flat * 2, ctx_at // 2, head_at])
    whole = full((STEPS, ROWS, 128))
    mixed, squares, rows_dec, reads = pl.pallas_call(
        decode_kernel,
        grid_spec=pltpu.PrefetchScalarGridSpec(
            num_scalar_prefetch=1,
            grid=(STEPS,),
            in_specs=[smem] * 4 + [full(state_cache.reshape(-1, 128, STATE).shape),
                                   pl.BlockSpec((lines, STATE), lambda k, *_: (k, 0)),
                                   whole, full((STEPS, 2, ROWS)), full((1, ROWS)), whole],
            out_specs=[whole, full((8, ROWS)), full((24 * STEPS, 128)),
                       pl.BlockSpec((8, STATE), lambda k, *_: (k, 0))],
            scratch_shapes=[pltpu.VMEM((ROWS, ROWS), BF16)]
            + [pltpu.VMEM((STEPS, ROWS, STATE), BF16)] * 3
            + [pltpu.VMEM((STEPS, ROWS, 128), F32)],
        ),
        out_shape=[jax.ShapeDtypeStruct((STEPS, ROWS, 128), F32),
                   jax.ShapeDtypeStruct((8, ROWS), F32),
                   jax.ShapeDtypeStruct((24 * STEPS, 128), F32),
                   jax.ShapeDtypeStruct((8 * STEPS, STATE), F32)],
        compiler_params=params(),
        cost_estimate=cost(2 * 10**9, 6 * 2**20),
        name="decode",
    )(at, a_log, dt_bias, d_skip, traj_slot, far(state_cache.reshape(-1, 128, STATE)),
      far(bc_decode.reshape(STEPS * lines, STATE)), far(x_decode),
      far(jnp.swapaxes(dt_decode, 1, 2)), traj, far(z_decode))
    rows_dec = lax.ppermute(rows_dec, ("ctx", "head"), owners)

    enter, first = pl.pallas_call(
        scan_kernel,
        in_specs=[vmem] * 4,
        out_specs=[vmem] * 2,
        out_shape=[pltpu.HBM((RANKS, STATE + 8, 128), F32),
                   jax.ShapeDtypeStruct((8 * STEPS, 128), F32)],
        compiler_params=params(16),
        cost_estimate=cost(10**8, 4 * 2**20),
        name="scan",
    )(got, prior, reads, rows_dec)
    enter = lax.all_to_all(enter, "ctx", 0, 0)

    for away in ((1, 2, 3), (4, 8, 12)):
        squares = squares + sum(
            lax.ppermute(squares, ("ctx", "head"), [(i, i ^ d) for i in range(128)]) for d in away)

    enter, squares = lax.optimization_barrier((enter, squares))
    first = pl.pallas_call(
        rows_kernel,
        grid_spec=pltpu.PrefetchScalarGridSpec(
            num_scalar_prefetch=1,
            grid=(1,),
            in_specs=[pl.BlockSpec((RANKS, 8, 128), lambda b, at: (0, STATE // 8, 0)),
                      full((8 * STEPS, 128)), pl.BlockSpec((1, 128), lambda b, at: (0, at[0]))],
            out_specs=full((8 * STEPS, 128)),
        ),
        out_shape=jax.ShapeDtypeStruct((8 * STEPS, 128), BF16),
        compiler_params=params(),
        cost_estimate=cost(10**7, 2**18),
        name="rows",
    )(jnp.reshape(head_at * RANKS + ctx_at, (1,)), enter, first, far(norm_gain.reshape(1, -1)))
    first = lax.ppermute(first, ("ctx", "head"), [(b, a) for a, b in owners])

    prefill_out = gate_call(here, far(yl), far(car), far(bc), far(bt), far(er), enter, far(z_tokens),
                            far(norm_gain.reshape(1, -1)))

    decode_out = pl.pallas_call(
        norm_kernel,
        grid_spec=pltpu.PrefetchScalarGridSpec(
            num_scalar_prefetch=1,
            grid=(1,),
            in_specs=[full((STEPS, ROWS, 128)), full((8, ROWS)), full((8 * STEPS, 128)),
                      full((1, ROWS)), pl.BlockSpec((1, 128), lambda b, at: (0, at[0]))],
            out_specs=full((STEPS, ROWS, 128)),
        ),
        out_shape=jax.ShapeDtypeStruct((STEPS, ROWS, 128), BF16),
        compiler_params=params(),
        cost_estimate=cost(10**7, 2**19),
        name="norm",
    )(jnp.reshape(flat, (1,)), mixed, squares, first, traj,
      far(norm_gain.reshape(1, -1)))
    return (prefill_out, decode_out)


def solution(mesh):
    in_specs = (
        P("ctx", "head"),
        P("ctx", None, "head", None),
        P("ctx", "head"),
        P("ctx", "head"),
        P(None, "head"),
        P(None, None, "head", None),
        P("head"),
        P(None, "head", None),
        P(),
        P(),
        P(),
        P(),
        P(None, ("ctx", "head"), None, None),
        P(),
        P(),
        P(None, None, ("ctx", "head")),
        P(),
        P(None, None, ("ctx", "head")),
        P(None, None, ("ctx", "head")),
    )
    out_specs = (P("ctx", "head"), P(None, None, ("ctx", "head")))
    return jax.shard_map(local, mesh=mesh, in_specs=in_specs, out_specs=out_specs, check_vma=False)
```

```python
import jax
import jax.numpy as jnp
from jax import lax
from jax.experimental import pallas as pl
from jax.experimental.pallas import tpu as pltpu
from jax.sharding import PartitionSpec as P

BLOCK = 128
HEAD = 64
STATE = 256
HEADS = 256
SPAN = 32
WIDTH = SPAN * HEAD
RANKS = 16
ROWS = 128
STEPS = 4
SUBS = 2
QUAD = 256
EPSILON = 1e-05
LOG2E = 1.4426950408889634
F32 = jnp.float32
BF16 = jnp.bfloat16


def dot(a, b, dims=((1,), (0,))):
    return lax.dot_general(a, b, (dims, ((), ())), preferred_element_type=F32)


def halves(v):
    hi = v.astype(BF16)
    return hi, (v - hi.astype(F32)).astype(BF16)


def thirds(v):
    hi, mid = halves(v)
    return hi, mid, (v - hi.astype(F32) - mid.astype(F32)).astype(BF16)


def softplus(v):
    return jnp.maximum(v, 0.0) + jnp.log1p(jnp.exp(-jnp.abs(v)))


def silu(v):
    h = 0.5 * v
    return h + h * jnp.tanh(h)


def iota(shape, dim):
    return lax.broadcasted_iota(jnp.int32, shape, dim)


def fill_expander(ref):
    shape = (2 * SPAN, WIDTH)
    ref[...] = jnp.where(iota(shape, 1) // HEAD == iota(shape, 0) % SPAN, 1.0, 0.0).astype(BF16)


def conv(block, before, taps):
    joined = jnp.concatenate([before, block], 0)
    late = pltpu.roll(joined, 1, 0)
    older = taps[1:2] * joined + taps[0:1] * late
    h = taps[4:5] + pltpu.roll(older, 2, 0)[8:]
    h = h + taps[2:3] * late[8:] + taps[3:4] * block
    return (h + h * jnp.tanh(h)).astype(BF16)


def own_heads(head_at, alog_ref, bias_ref, skip_ref):
    rows = jnp.concatenate([alog_ref[...], bias_ref[...]] + [skip_ref[...]] * 6, 0)
    shape = (SPAN, rows.shape[1])
    mine = jnp.where(iota(shape, 1) == iota(shape, 0) + head_at * SPAN, 1.0, 0.0).astype(BF16)
    return sum(dot(mine, piece, ((1,), (1,))) for piece in thirds(rows))


def spread_heads(rows, spread):
    return dot(rows, spread)


def over_channels(rows, q):
    left = iota((rows.shape[0], 128), 1) < HEAD
    first = q * QUAD // HEAD
    return jnp.concatenate(
        [jnp.where(left, rows[:, h:h + 1], rows[:, h + 1:h + 2])
         for h in range(first, first + QUAD // HEAD, 2)], 1)


def pair_halves(rows):
    return jnp.concatenate(halves(rows), 1)


def prep_kernel(at_ref, x_ref, bc_ref, edge_ref, dt_ref, alog_ref, bias_ref, skip_ref, cw_ref, cb_ref,
                bw_ref, bb_ref, xc_ref, car_ref, bco_ref, bt_ref, rdt_ref, er_ref, send_ref,
                prevx, state, spread, wx, wbc, factors, decays):
    step = pl.program_id(0)
    blocks = rdt_ref.shape[0]

    @pl.when(step == 0)
    def _():
        fill_expander(spread)
        own = own_heads(at_ref[0], alog_ref, bias_ref, skip_ref)
        state[...] = jnp.zeros_like(state)
        wx[0:4, :] = cw_ref[...].astype(F32) * 0.5
        offset = cb_ref[...].astype(F32) * 0.5
        for i in range(WIDTH // 128):
            wx[4:5, i * 128:(i + 1) * 128] = offset[i:i + 1]
        taps = bw_ref[...].astype(F32) * 0.5
        offset = bb_ref[...].astype(F32) * 0.5
        for i in range(2):
            wbc[0:4, i * STATE:(i + 1) * STATE] = taps[:, i, :]
            wbc[4:5, i * STATE:(i + 1) * STATE] = offset[i:i + 1]
        edge = edge_ref[...].astype(F32)
        prevx[...] = jnp.zeros_like(prevx)
        prevx[5:8, :] = edge[:, :WIDTH]
        before = jnp.concatenate([jnp.zeros((5, 2 * STATE), F32), edge[:, WIDTH:]], 0)

        dt = softplus(dt_ref[...] + own[:, 1:2])
        log = dt * (jnp.exp(own[:, 0:1]) * (-LOG2E))
        spans = [slice(b * BLOCK, (b + 1) * BLOCK) for b in range(blocks)]
        dt = jnp.concatenate([dt[:, span] for span in spans], 0)
        log = jnp.concatenate([log[:, span] for span in spans], 0)
        tri = jnp.where(iota((BLOCK, BLOCK), 0) <= iota((BLOCK, BLOCK), 1), 1.0, 0.0).astype(BF16)
        r = sum(dot(piece, tri) for piece in thirds(log))
        r_last = r[:, BLOCK - 1:BLOCK]
        tail = jnp.exp2(r_last - r) * dt
        er = jnp.exp2(r)
        wide = jnp.broadcast_to(r_last, r.shape)
        decay = jnp.exp2(wide)
        whole = jnp.zeros((SPAN, BLOCK), F32)
        for b in range(blocks):
            heads = slice(b * SPAN, (b + 1) * SPAN)
            rdt_ref[b] = jnp.concatenate([r[heads], dt[heads]], 0)
            er_ref[b] = pair_halves(er[heads].T)
            factors[b] = tail[heads].T
            rows = spread_heads(pair_halves(decay[heads].T[:16]), spread[...])
            decays[b:b + 1, :] = rows[0:1]
            whole = whole + wide[heads]
        rows = spread_heads(pair_halves(jnp.exp2(whole).T[:16]), spread[...])
        decays[blocks:blocks + 8, :] = rows[0:8]
        for b in range(blocks):
            bc_in = bc_ref[spans[b], :].astype(F32)
            bc = conv(bc_in, before, wbc[...])
            before = bc_in[BLOCK - 8:]
            bco_ref[spans[b], :] = bc
            bt_ref[b] = bc[:, :STATE].astype(F32).T.astype(BF16)

    for sub in range(x_ref.shape[0] // BLOCK):
        block_at = step * (x_ref.shape[0] // BLOCK) + sub
        span = slice(sub * BLOCK, (sub + 1) * BLOCK)
        b_across = bt_ref[block_at]
        lhs = factors[block_at]
        for q in range(WIDTH // QUAD):
            cols = slice(q * QUAD, (q + 1) * QUAD)
            x_in = x_ref[span, cols].astype(F32)
            xc = conv(x_in, prevx[:, cols], wx[:, cols])
            prevx[:, cols] = x_in[BLOCK - 8:]
            xc_ref[span, cols] = xc
            carried = (xc.astype(F32) * over_channels(lhs, q)).astype(BF16)
            car_ref[span, cols] = carried
            fresh = dot(b_across, carried)
            state[:, cols] = state[:, cols] * decays[pl.ds(block_at, 1), cols] + fresh

    @pl.when(step == pl.num_programs(0) - 1)
    def _():
        for c in range(RANKS):
            cols = slice(c * 128, (c + 1) * 128)
            send_ref[c, 0:STATE, :] = state[:, cols]
            send_ref[c, STATE:, :] = decays[blocks:blocks + 8, cols]


def inner_kernel(at_ref, xc_ref, bc_ref, rdt_ref, alog_ref, bias_ref, skip_ref, yl_ref, skip):
    @pl.when(pl.program_id(0) == 0)
    def _():
        spread = jnp.where(
            iota((SPAN, WIDTH), 1) // HEAD == iota((SPAN, WIDTH), 0), 1.0, 0.0).astype(BF16)
        own = own_heads(at_ref[0], alog_ref, bias_ref, skip_ref)
        skip[...] = sum(dot(p, spread, ((0,), (0,))) for p in thirds(own))

    b_now = bc_ref[:, :STATE]
    c_now = bc_ref[:, STATE:]
    scores = dot(c_now, b_now, ((1,), (1,)))
    scores = jnp.where(iota((BLOCK, BLOCK), 1) <= iota((BLOCK, BLOCK), 0), scores, 0.0)
    along = rdt_ref[0]
    r = along.T
    left = iota((BLOCK, 128), 1) < HEAD

    for q in range(WIDTH // QUAD):
        cols = slice(q * QUAD, (q + 1) * QUAD)
        xq = xc_ref[:, cols]
        parts = []
        for pair in range(2):
            weights = []
            for h in (4 * q + 2 * pair, 4 * q + 2 * pair + 1):
                gap = jnp.minimum(r[:, h:h + 1] - along[h:h + 1, :], 0.0)
                weight = jnp.exp2(gap) * (scores * along[SPAN + h:SPAN + h + 1, :])
                weights.append(weight.astype(BF16))
            xp = xq[:, pair * 128:(pair + 1) * 128]
            none = jnp.zeros_like(xp)
            rhs = jnp.concatenate([jnp.where(left, xp, none), jnp.where(left, none, xp)], 0)
            parts.append(dot(jnp.concatenate(weights, 1), rhs))
        out = jnp.concatenate(parts, 1) + skip[2:3, cols] * xq.astype(F32)
        yl_ref[:, cols] = out.astype(BF16)


def chosen_rows(traj):
    hit = jnp.broadcast_to(jnp.where(traj == 0, 1.0, 0.0), (8, ROWS))
    ahead = jnp.where(iota((ROWS, ROWS), 0) < iota((ROWS, ROWS), 1), 1.0, 0.0).astype(BF16)
    rank = dot(hit.astype(BF16), ahead)
    return jnp.where((rank == iota((8, ROWS), 0).astype(F32)) & (hit > 0.5), 1.0, 0.0)


def scan_kernel(got_ref, prior_ref, reads_ref, rows_ref, enter_ref, mixed_ref):
    held = prior_ref[...].astype(F32).T
    for c in range(RANKS):
        enter_ref[c, 0:STATE, :] = held
        held = held * got_ref[c, STATE:STATE + 1, :] + got_ref[c, 0:STATE, :]
    hi, lo = halves(held)
    reads = reads_ref[...].astype(BF16)
    count = 8 * STEPS
    y = rows_ref[0:count] + rows_ref[count:2 * count] * (dot(reads, hi) + dot(reads, lo))
    m = y * rows_ref[2 * count:]
    mixed_ref[...] = m
    sums = row_sums(jnp.concatenate([m * m, jnp.zeros((128 - count, 128), F32)], 0))
    for c in range(RANKS):
        enter_ref[c, STATE:, :] = sums


def row_sums(v):
    ones = jnp.ones((8, v.shape[1]), BF16)
    hi, lo = halves(v)
    return dot(ones, hi, ((1,), (1,))) + dot(ones, lo, ((1,), (1,)))


def scales(sums):
    scale = lax.rsqrt(sums * (1.0 / WIDTH) + EPSILON)
    return jnp.broadcast_to(scale, (128, 128)).T


def rows_kernel(at_ref, sums_ref, mixed_ref, gain_ref, rows_ref):
    total = sums_ref[0]
    for c in range(1, RANKS):
        total = total + sums_ref[c]
    scale = scales(total[0:1])[:8 * STEPS]
    rows_ref[...] = (mixed_ref[...] * scale * gain_ref[...]).astype(BF16)


def out_kernel(at_ref, yl_ref, car_ref, c_ref, bt_ref, er_ref, in_ref, z_ref, gain_ref, out_ref,
               spread, state, mixed):
    @pl.when(pl.program_id(0) == 0)
    def _():
        fill_expander(spread)
        for c in range(RANKS):
            state[:, c * 128:(c + 1) * 128] = in_ref[c, 0:STATE, :]

    subs = yl_ref.shape[0] // BLOCK
    scale = None
    for sub in range(subs + 1):
        span = slice(sub * BLOCK, (sub + 1) * BLOCK)
        done = slice((sub - 1) * BLOCK, sub * BLOCK)
        total = jnp.zeros((BLOCK, 128), F32)
        for q in range(WIDTH // QUAD):
            cols = slice(q * QUAD, (q + 1) * QUAD)
            if sub < subs:
                factor = spread_heads(er_ref[sub], spread[:, cols])
                held = state[:, cols]
                y = yl_ref[span, cols].astype(F32) + dot(c_ref[span, :], held.astype(BF16)) * factor
                fresh = dot(bt_ref[sub], car_ref[span, cols])
                state[:, cols] = held * factor[BLOCK - 1:BLOCK] + fresh
                m = y * silu(z_ref[span, cols].astype(F32))
                mixed[span, cols] = m
                sq = m * m
                total = total + sum(sq[:, i:i + 128] for i in range(0, QUAD, 128))
            if sub > 0:
                out_ref[done, cols] = (mixed[done, cols] * scale * gain_ref[:, cols]).astype(BF16)
        mean = jnp.sum(total, axis=1, keepdims=True) * (1.0 / WIDTH)
        scale = lax.rsqrt(mean + EPSILON)


def two_heads(at_ref, ref):
    first = at_ref[0]
    lane = iota((1, 128), 1)
    return jnp.where(lane < HEAD, ref[first], ref[first + 1])


def decode_kernel(at_ref, alog_ref, bias_ref, skip_ref, slot_ref, cache_ref, bc_ref, x_ref, dt_ref,
                  traj_ref, z_ref, m_ref, sq_ref, rows_ref, reads_ref,
                  order, held_b, held_c, sorted_c, reads):
    step = pl.program_id(0)

    @pl.when(step == 0)
    def _():
        traj = jnp.broadcast_to(traj_ref[...].astype(F32), (ROWS, ROWS))
        sub, lane = iota((ROWS, ROWS), 0), iota((ROWS, ROWS), 1)
        rank = jnp.sum(jnp.where((traj == traj.T) & (sub < lane), 1.0, 0.0), axis=0, keepdims=True)
        place = traj_ref[...].astype(F32) * 4.0 + rank
        order[...] = jnp.where(sub.astype(F32) == place, 1.0, 0.0).astype(BF16)

    shape = (96, 512)
    out, line = iota(shape, 0), iota(shape, 1)
    group = jnp.where(out < 64, at_ref[1], at_ref[2])
    wanted = (out % 32) * 16 + jnp.where(out < 32, 0, 8) + group
    pick = jnp.where(line == wanted, 1.0, 0.0).astype(BF16)
    prefill_c = []
    for g in range(ROWS // 32):
        got = dot(pick, bc_ref[g * 512:(g + 1) * 512, :]).astype(BF16)
        held_b[step, g * 32:(g + 1) * 32, :] = got[0:32]
        held_c[step, g * 32:(g + 1) * 32, :] = got[32:64]
        prefill_c.append(got[64:96])
    sorted_c[step] = dot(order[...], held_c[step]).astype(BF16)
    chosen = chosen_rows(traj_ref[...]).astype(BF16)
    reads_ref[...] = dot(chosen, jnp.concatenate(prefill_c, 0))

    @pl.when(step == STEPS - 1)
    def _():
        for g in range(ROWS // 16):
            lhs = jnp.concatenate([sorted_c[k, g * 16:(g + 1) * 16, :] for k in range(STEPS)], 0)
            row = iota((16 * STEPS, 128), 0) % 16 // 4
            out = jnp.zeros((16 * STEPS, 128), F32)
            for i in range(4):
                if g == 0 and i == 0:
                    continue
                got = dot(lhs, cache_ref[slot_ref[4 * g + i]], ((1,), (1,)))
                out = jnp.where(row == i, got, out)
            for k in range(STEPS):
                reads[k, g * 16:(g + 1) * 16, :] = out[k * 16:(k + 1) * 16]

        rate = jnp.exp(two_heads(at_ref, alog_ref)) * (-LOG2E)
        bias = two_heads(at_ref, bias_ref)
        skip = two_heads(at_ref, skip_ref)
        upper = iota((128, ROWS), 0) < HEAD
        sq_ref[...] = jnp.zeros_like(sq_ref)
        total = jnp.ones((ROWS, 128), F32)
        pushed = []
        for k in range(STEPS):
            raw = dt_ref[k]
            dt = softplus(jnp.where(upper, raw[0:1, :], raw[1:2, :]).T + bias)
            x_now = x_ref[k].astype(F32)
            decay = jnp.exp2(dt * rate)
            total = total * decay
            pushed = [p * decay for p in pushed] + [dt * x_now]
            hi, lo = halves(reads[k])
            back = dot(order[...], hi, ((0,), (0,))) + dot(order[...], lo, ((0,), (0,)))
            y = total * back + skip * x_now
            c_now = held_c[k].astype(F32)
            for j in range(k + 1):
                met = jnp.sum(held_b[j].astype(F32) * c_now, axis=1, keepdims=True)
                y = y + pushed[j] * met
            gate = silu(z_ref[k].astype(F32))
            m = y * gate
            m_ref[k] = m
            sq_ref[k:k + 1, :] = row_sums(m * m)[0:1]
            for i, part in enumerate((y, total, gate)):
                hi, lo = halves(part)
                at = 8 * (STEPS * i + k)
                rows_ref[at:at + 8, :] = dot(chosen, hi) + dot(chosen, lo)


def norm_kernel(at_ref, m_ref, sq_ref, traj_ref, gain_ref, out_ref, chosen_ref):
    chosen = chosen_rows(traj_ref[...])
    chosen_ref[...] = chosen
    first = dot(chosen.astype(BF16), jnp.ones((8, 128), BF16), ((0,), (0,))) > 0.5
    for k in range(STEPS):
        out = m_ref[k] * scales(sq_ref[k:k + 1, :]) * gain_ref[...]
        out_ref[k] = jnp.where(first, 0.0, out).astype(BF16)


def patch_kernel(rest_ref, rows_ref, chosen_ref, out_ref):
    chosen = chosen_ref[...].astype(BF16)
    for k in range(STEPS):
        rows = dot(chosen, rows_ref[k * 8:(k + 1) * 8, :].astype(BF16), ((0,), (0,)))
        out_ref[k] = (rest_ref[k].astype(F32) + rows).astype(BF16)


def full(shape):
    return pl.BlockSpec(shape, lambda *_: (0,) * len(shape))


def far(x):
    return pltpu.with_memory_space_constraint(x, pltpu.HBM)


def params(mib=24):
    return pltpu.CompilerParams(vmem_limit_bytes=mib * 2**20)


def cost(flops, nbytes):
    return pl.CostEstimate(flops=flops, bytes_accessed=nbytes, transcendentals=0)


def block_rows(width):
    return pl.BlockSpec((BLOCK, width), lambda b, *_: (b, 0))


def block_times():
    return pl.BlockSpec((1, 2 * SPAN, BLOCK), lambda b, *_: (b, 0, 0))


def prep_call(here, x, *rest):
    tokens = x.shape[0]
    blocks = tokens // BLOCK
    rows = pl.BlockSpec((SUBS * BLOCK, WIDTH), lambda b, *_: (b, 0))
    shapes = [((tokens, WIDTH), BF16), ((tokens, WIDTH), BF16), ((tokens, 2 * STATE), BF16),
              ((blocks, STATE, BLOCK), BF16), ((blocks, 2 * SPAN, BLOCK), F32),
              ((blocks, BLOCK, 2 * SPAN), BF16), ((RANKS, STATE + 8, 128), F32)]
    return pl.pallas_call(
        prep_kernel,
        grid_spec=pltpu.PrefetchScalarGridSpec(
            num_scalar_prefetch=1,
            grid=(blocks // SUBS,),
            in_specs=[rows, full((tokens, 2 * STATE)), full((3, WIDTH + 2 * STATE)),
                      full((SPAN, tokens)), *[full((1, HEADS))] * 3, full((4, WIDTH)),
                      full((WIDTH // 128, 128)), full((4, 2, STATE)), full((2, STATE))],
            out_specs=[rows, rows] + [full(shape) for shape, _ in shapes[2:]],
            scratch_shapes=[pltpu.VMEM((8, WIDTH), F32), pltpu.VMEM((STATE, WIDTH), F32),
                            pltpu.VMEM((2 * SPAN, WIDTH), BF16), pltpu.VMEM((8, WIDTH), F32),
                            pltpu.VMEM((8, 2 * STATE), F32),
                            pltpu.VMEM((blocks, BLOCK, SPAN), F32),
                            pltpu.VMEM((blocks + 8, WIDTH), F32)],
        ),
        out_shape=[pltpu.HBM(shape, dtype) for shape, dtype in shapes],
        compiler_params=params(),
        cost_estimate=cost(8 * 10**9, 20 * 2**20),
        name="prep",
    )(here, x, *rest)


def inner_call(here, xc, *rest):
    tokens = xc.shape[0]
    blocks = tokens // BLOCK
    rows, times, head_specs = block_rows, block_times(), [full((1, HEADS))] * 3
    return pl.pallas_call(
        inner_kernel,
        grid_spec=pltpu.PrefetchScalarGridSpec(
            num_scalar_prefetch=1,
            grid=(blocks,),
            in_specs=[rows(WIDTH), rows(2 * STATE), times, *head_specs],
            out_specs=rows(WIDTH),
            scratch_shapes=[pltpu.VMEM((8, WIDTH), F32)],
        ),
        out_shape=pltpu.HBM((tokens, WIDTH), BF16),
        compiler_params=params(),
        cost_estimate=cost(8 * 10**9, 20 * 2**20),
        name="inner",
    )(here, xc, *rest)


def gate_call(here, yl, *rest):
    tokens = yl.shape[0]
    rows = pl.BlockSpec((SUBS * BLOCK, WIDTH), lambda b, *_: (b, 0))
    return pl.pallas_call(
        out_kernel,
        grid_spec=pltpu.PrefetchScalarGridSpec(
            num_scalar_prefetch=1,
            grid=(tokens // BLOCK // SUBS,),
            in_specs=[rows, rows, pl.BlockSpec((SUBS * BLOCK, STATE), lambda b, *_: (b, 1)),
                      pl.BlockSpec((SUBS, STATE, BLOCK), lambda b, *_: (b, 0, 0)),
                      pl.BlockSpec((SUBS, BLOCK, 2 * SPAN), lambda b, *_: (b, 0, 0)),
                      full((RANKS, STATE + 8, 128)), rows,
                      pl.BlockSpec((1, WIDTH), lambda b, at: (0, at[0]))],
            out_specs=rows,
            scratch_shapes=[pltpu.VMEM((2 * SPAN, WIDTH), BF16), pltpu.VMEM((STATE, WIDTH), F32),
                            pltpu.VMEM((SUBS * BLOCK, WIDTH), F32)],
        ),
        out_shape=jax.ShapeDtypeStruct((tokens, WIDTH), BF16),
        compiler_params=params(),
        cost_estimate=cost(4 * 10**9, 16 * 2**20),
        name="gate",
    )(here, yl, *rest)


def local(x_tokens, bc_tokens, z_tokens, dt_tokens, conv_x, conv_bc, bias_x, bias_bc, a_log, dt_bias,
          d_skip, norm_gain, state_cache, traj_slot, row_traj, x_decode, bc_decode, z_decode,
          dt_decode):
    ctx_at = lax.axis_index("ctx").astype(jnp.int32)
    head_at = lax.axis_index("head").astype(jnp.int32)
    flat = ctx_at * 8 + head_at
    tokens = x_tokens.shape[0]
    vmem = pl.BlockSpec(memory_space=pltpu.VMEM)
    smem = pl.BlockSpec(memory_space=pltpu.SMEM)

    bc_flat = bc_tokens.reshape(tokens, 2 * STATE)
    edge = jnp.concatenate(
        [x_tokens[tokens - 3:], bc_tokens[tokens - 3:].reshape(3, 2 * STATE)], 1)
    edge = lax.ppermute(edge, "ctx", [(i, i + 1) for i in range(RANKS - 1)])
    owners = [(16 * g + c, 8 * c + g) for c in range(RANKS) for g in range(8)]

    traj = far(row_traj.reshape(1, ROWS))
    here = jnp.reshape(head_at, (1,))
    per_head = [far(v.reshape(1, -1)) for v in (a_log, dt_bias, d_skip)]

    xc, car, bc, bt, rdt, er, send = prep_call(
        here, far(x_tokens), bc_flat, edge, far(dt_tokens.T), *per_head, far(conv_x),
        far(bias_x.reshape(-1, 128)), far(conv_bc.reshape(4, 2, STATE)),
        far(bias_bc.reshape(2, STATE)))

    got = lax.all_to_all(send, "ctx", 0, 0)

    yl = inner_call(here, far(xc), far(bc), far(rdt), *per_head)
    got, yl = lax.optimization_barrier((got, yl))

    lines = ROWS * 16
    at = jnp.stack([flat * 2, ctx_at // 2, head_at])
    whole = full((STEPS, ROWS, 128))
    mixed, squares, rows_dec, reads = pl.pallas_call(
        decode_kernel,
        grid_spec=pltpu.PrefetchScalarGridSpec(
            num_scalar_prefetch=1,
            grid=(STEPS,),
            in_specs=[smem] * 4 + [full(state_cache.reshape(-1, 128, STATE).shape),
                                   pl.BlockSpec((lines, STATE), lambda k, *_: (k, 0)),
                                   whole, full((STEPS, 2, ROWS)), full((1, ROWS)), whole],
            out_specs=[whole, full((8, ROWS)), full((24 * STEPS, 128)),
                       pl.BlockSpec((8, STATE), lambda k, *_: (k, 0))],
            scratch_shapes=[pltpu.VMEM((ROWS, ROWS), BF16)]
            + [pltpu.VMEM((STEPS, ROWS, STATE), BF16)] * 3
            + [pltpu.VMEM((STEPS, ROWS, 128), F32)],
        ),
        out_shape=[jax.ShapeDtypeStruct((STEPS, ROWS, 128), F32),
                   jax.ShapeDtypeStruct((8, ROWS), F32),
                   jax.ShapeDtypeStruct((24 * STEPS, 128), F32),
                   jax.ShapeDtypeStruct((8 * STEPS, STATE), F32)],
        compiler_params=params(),
        cost_estimate=cost(2 * 10**9, 6 * 2**20),
        name="decode",
    )(at, a_log, dt_bias, d_skip, traj_slot, far(state_cache.reshape(-1, 128, STATE)),
      far(bc_decode.reshape(STEPS * lines, STATE)), far(x_decode),
      far(jnp.swapaxes(dt_decode, 1, 2)), traj, far(z_decode))
    rows_dec, slots = lax.optimization_barrier((rows_dec, traj_slot))
    rows_dec = lax.ppermute(rows_dec, ("ctx", "head"), owners)
    prior = state_cache[slots[0]].reshape(128, STATE)
    prior = lax.ppermute(prior, ("ctx", "head"), owners)

    enter, first = pl.pallas_call(
        scan_kernel,
        in_specs=[vmem] * 4,
        out_specs=[vmem] * 2,
        out_shape=[pltpu.HBM((RANKS, STATE + 8, 128), F32),
                   jax.ShapeDtypeStruct((8 * STEPS, 128), F32)],
        compiler_params=params(16),
        cost_estimate=cost(10**8, 4 * 2**20),
        name="scan",
    )(got, prior, reads, rows_dec)
    enter = lax.all_to_all(enter, "ctx", 0, 0)

    for away in ((1, 2, 3), (4, 8, 12)):
        squares = squares + sum(
            lax.ppermute(squares, ("ctx", "head"), [(i, i ^ d) for i in range(128)]) for d in away)

    rest, chosen = pl.pallas_call(
        norm_kernel,
        grid_spec=pltpu.PrefetchScalarGridSpec(
            num_scalar_prefetch=1,
            grid=(1,),
            in_specs=[full((STEPS, ROWS, 128)), full((8, ROWS)), full((1, ROWS)),
                      pl.BlockSpec((1, 128), lambda b, at: (0, at[0]))],
            out_specs=[full((STEPS, ROWS, 128)), full((8, ROWS))],
        ),
        out_shape=[jax.ShapeDtypeStruct((STEPS, ROWS, 128), BF16),
                   jax.ShapeDtypeStruct((8, ROWS), F32)],
        compiler_params=params(),
        cost_estimate=cost(10**7, 2**19),
        name="norm",
    )(jnp.reshape(flat, (1,)), mixed, squares, traj, far(norm_gain.reshape(1, -1)))
    enter, rest = lax.optimization_barrier((enter, rest))
    first = pl.pallas_call(
        rows_kernel,
        grid_spec=pltpu.PrefetchScalarGridSpec(
            num_scalar_prefetch=1,
            grid=(1,),
            in_specs=[pl.BlockSpec((RANKS, 8, 128), lambda b, at: (0, STATE // 8, 0)),
                      full((8 * STEPS, 128)), pl.BlockSpec((1, 128), lambda b, at: (0, at[0]))],
            out_specs=full((8 * STEPS, 128)),
        ),
        out_shape=jax.ShapeDtypeStruct((8 * STEPS, 128), BF16),
        compiler_params=params(),
        cost_estimate=cost(10**7, 2**18),
        name="rows",
    )(jnp.reshape(head_at * RANKS + ctx_at, (1,)), enter, first, far(norm_gain.reshape(1, -1)))
    first = lax.ppermute(first, ("ctx", "head"), [(b, a) for a, b in owners])

    prefill_out = gate_call(here, far(yl), far(car), far(bc), far(bt), far(er), enter, far(z_tokens),
                            far(norm_gain.reshape(1, -1)))

    decode_out = pl.pallas_call(
        patch_kernel,
        in_specs=[vmem] * 3,
        out_specs=vmem,
        out_shape=jax.ShapeDtypeStruct((STEPS, ROWS, 128), BF16),
        compiler_params=params(16),
        cost_estimate=cost(10**7, 2**18),
        name="patch",
    )(rest, first, chosen)
    return (prefill_out, decode_out)


def solution(mesh):
    in_specs = (
        P("ctx", "head"),
        P("ctx", None, "head", None),
        P("ctx", "head"),
        P("ctx", "head"),
        P(None, "head"),
        P(None, None, "head", None),
        P("head"),
        P(None, "head", None),
        P(),
        P(),
        P(),
        P(),
        P(None, ("ctx", "head"), None, None),
        P(),
        P(),
        P(None, None, ("ctx", "head")),
        P(),
        P(None, None, ("ctx", "head")),
        P(None, None, ("ctx", "head")),
    )
    out_specs = (P("ctx", "head"), P(None, None, ("ctx", "head")))
    return jax.shard_map(local, mesh=mesh, in_specs=in_specs, out_specs=out_specs, check_vma=False)
```

```python
import jax
import jax.numpy as jnp
from jax import lax
from jax.experimental import pallas as pl
from jax.experimental.pallas import tpu as pltpu
from jax.sharding import PartitionSpec as P

BLOCK = 128
HEAD = 64
STATE = 256
HEADS = 256
SPAN = 32
WIDTH = SPAN * HEAD
RANKS = 16
ROWS = 128
STEPS = 4
SUBS = 2
QUAD = 256
EPSILON = 1e-05
LOG2E = 1.4426950408889634
F32 = jnp.float32
BF16 = jnp.bfloat16


def dot(a, b, dims=((1,), (0,))):
    return lax.dot_general(a, b, (dims, ((), ())), preferred_element_type=F32)


def halves(v):
    hi = v.astype(BF16)
    return hi, (v - hi.astype(F32)).astype(BF16)


def thirds(v):
    hi, mid = halves(v)
    return hi, mid, (v - hi.astype(F32) - mid.astype(F32)).astype(BF16)


def softplus(v):
    return jnp.maximum(v, 0.0) + jnp.log1p(jnp.exp(-jnp.abs(v)))


def silu(v):
    h = 0.5 * v
    return h + h * jnp.tanh(h)


def iota(shape, dim):
    return lax.broadcasted_iota(jnp.int32, shape, dim)


def fill_expander(ref):
    shape = (2 * SPAN, WIDTH)
    ref[...] = jnp.where(iota(shape, 1) // HEAD == iota(shape, 0) % SPAN, 1.0, 0.0).astype(BF16)


def conv(block, before, taps):
    joined = jnp.concatenate([before, block], 0)
    late = pltpu.roll(joined, 1, 0)
    older = taps[1:2] * joined + taps[0:1] * late
    h = taps[4:5] + pltpu.roll(older, 2, 0)[8:]
    h = h + taps[2:3] * late[8:] + taps[3:4] * block
    return (h + h * jnp.tanh(h)).astype(BF16)


def own_heads(head_at, alog_ref, bias_ref, skip_ref):
    rows = jnp.concatenate([alog_ref[...], bias_ref[...]] + [skip_ref[...]] * 6, 0)
    shape = (SPAN, rows.shape[1])
    mine = jnp.where(iota(shape, 1) == iota(shape, 0) + head_at * SPAN, 1.0, 0.0).astype(BF16)
    return sum(dot(mine, piece, ((1,), (1,))) for piece in thirds(rows))


def spread_heads(rows, spread):
    return dot(rows, spread)


def over_channels(rows, q):
    left = iota((rows.shape[0], 128), 1) < HEAD
    first = q * QUAD // HEAD
    return jnp.concatenate(
        [jnp.where(left, rows[:, h:h + 1], rows[:, h + 1:h + 2])
         for h in range(first, first + QUAD // HEAD, 2)], 1)


def pair_halves(rows):
    return jnp.concatenate(halves(rows), 1)


def prep_kernel(at_ref, x_ref, bc_ref, edge_ref, dt_ref, alog_ref, bias_ref, skip_ref, cw_ref, cb_ref,
                bw_ref, bb_ref, xc_ref, car_ref, bco_ref, bt_ref, rdt_ref, er_ref, send_ref,
                prevx, state, spread, wx, wbc, factors, decays):
    step = pl.program_id(0)
    blocks = rdt_ref.shape[0]

    @pl.when(step == 0)
    def _():
        fill_expander(spread)
        own = own_heads(at_ref[0], alog_ref, bias_ref, skip_ref)
        state[...] = jnp.zeros_like(state)
        wx[0:4, :] = cw_ref[...].astype(F32) * 0.5
        offset = cb_ref[...].astype(F32) * 0.5
        for i in range(WIDTH // 128):
            wx[4:5, i * 128:(i + 1) * 128] = offset[i:i + 1]
        taps = bw_ref[...].astype(F32) * 0.5
        offset = bb_ref[...].astype(F32) * 0.5
        for i in range(2):
            wbc[0:4, i * STATE:(i + 1) * STATE] = taps[:, i, :]
            wbc[4:5, i * STATE:(i + 1) * STATE] = offset[i:i + 1]
        edge = edge_ref[...].astype(F32)
        prevx[...] = jnp.zeros_like(prevx)
        prevx[5:8, :] = edge[:, :WIDTH]
        before = jnp.concatenate([jnp.zeros((5, 2 * STATE), F32), edge[:, WIDTH:]], 0)

        dt = softplus(dt_ref[...] + own[:, 1:2])
        log = dt * (jnp.exp(own[:, 0:1]) * (-LOG2E))
        spans = [slice(b * BLOCK, (b + 1) * BLOCK) for b in range(blocks)]
        dt = jnp.concatenate([dt[:, span] for span in spans], 0)
        log = jnp.concatenate([log[:, span] for span in spans], 0)
        tri = jnp.where(iota((BLOCK, BLOCK), 0) <= iota((BLOCK, BLOCK), 1), 1.0, 0.0).astype(BF16)
        r = sum(dot(piece, tri) for piece in thirds(log))
        r_last = r[:, BLOCK - 1:BLOCK]
        tail = jnp.exp2(r_last - r) * dt
        er = jnp.exp2(r)
        wide = jnp.broadcast_to(r_last, r.shape)
        decay = jnp.exp2(wide)
        whole = jnp.zeros((SPAN, BLOCK), F32)
        for b in range(blocks):
            heads = slice(b * SPAN, (b + 1) * SPAN)
            rdt_ref[b] = jnp.concatenate([r[heads], dt[heads]], 0)
            er_ref[b] = pair_halves(er[heads].T)
            factors[b] = tail[heads].T
            rows = spread_heads(pair_halves(decay[heads].T[:16]), spread[...])
            decays[b:b + 1, :] = rows[0:1]
            whole = whole + wide[heads]
        rows = spread_heads(pair_halves(jnp.exp2(whole).T[:16]), spread[...])
        decays[blocks:blocks + 8, :] = rows[0:8]
        for b in range(blocks):
            bc_in = bc_ref[spans[b], :].astype(F32)
            bc = conv(bc_in, before, wbc[...])
            before = bc_in[BLOCK - 8:]
            bco_ref[spans[b], :] = bc
            bt_ref[b] = bc[:, :STATE].astype(F32).T.astype(BF16)

    for sub in range(x_ref.shape[0] // BLOCK):
        block_at = step * (x_ref.shape[0] // BLOCK) + sub
        span = slice(sub * BLOCK, (sub + 1) * BLOCK)
        b_across = bt_ref[block_at]
        lhs = factors[block_at]
        for q in range(WIDTH // QUAD):
            cols = slice(q * QUAD, (q + 1) * QUAD)
            x_in = x_ref[span, cols].astype(F32)
            xc = conv(x_in, prevx[:, cols], wx[:, cols])
            prevx[:, cols] = x_in[BLOCK - 8:]
            xc_ref[span, cols] = xc
            carried = (xc.astype(F32) * over_channels(lhs, q)).astype(BF16)
            car_ref[span, cols] = carried
            fresh = dot(b_across, carried)
            state[:, cols] = state[:, cols] * decays[pl.ds(block_at, 1), cols] + fresh

    @pl.when(step == pl.num_programs(0) - 1)
    def _():
        for c in range(RANKS):
            cols = slice(c * 128, (c + 1) * 128)
            send_ref[c, 0:STATE, :] = state[:, cols]
            send_ref[c, STATE:, :] = decays[blocks:blocks + 8, cols]


def inner_kernel(at_ref, xc_ref, bc_ref, rdt_ref, alog_ref, bias_ref, skip_ref, yl_ref, skip):
    @pl.when(pl.program_id(0) == 0)
    def _():
        spread = jnp.where(
            iota((SPAN, WIDTH), 1) // HEAD == iota((SPAN, WIDTH), 0), 1.0, 0.0).astype(BF16)
        own = own_heads(at_ref[0], alog_ref, bias_ref, skip_ref)
        skip[...] = sum(dot(p, spread, ((0,), (0,))) for p in thirds(own))

    b_now = bc_ref[:, :STATE]
    c_now = bc_ref[:, STATE:]
    scores = dot(c_now, b_now, ((1,), (1,)))
    scores = jnp.where(iota((BLOCK, BLOCK), 1) <= iota((BLOCK, BLOCK), 0), scores, 0.0)
    along = rdt_ref[0]
    r = along.T
    left = iota((BLOCK, 128), 1) < HEAD

    for q in range(WIDTH // QUAD):
        cols = slice(q * QUAD, (q + 1) * QUAD)
        xq = xc_ref[:, cols]
        parts = []
        for pair in range(2):
            weights = []
            for h in (4 * q + 2 * pair, 4 * q + 2 * pair + 1):
                gap = jnp.minimum(r[:, h:h + 1] - along[h:h + 1, :], 0.0)
                weight = jnp.exp2(gap) * (scores * along[SPAN + h:SPAN + h + 1, :])
                weights.append(weight.astype(BF16))
            xp = xq[:, pair * 128:(pair + 1) * 128]
            none = jnp.zeros_like(xp)
            rhs = jnp.concatenate([jnp.where(left, xp, none), jnp.where(left, none, xp)], 0)
            parts.append(dot(jnp.concatenate(weights, 1), rhs))
        out = jnp.concatenate(parts, 1) + skip[2:3, cols] * xq.astype(F32)
        yl_ref[:, cols] = out.astype(BF16)


def chosen_rows(traj):
    hit = jnp.broadcast_to(jnp.where(traj == 0, 1.0, 0.0), (8, ROWS))
    ahead = jnp.where(iota((ROWS, ROWS), 0) < iota((ROWS, ROWS), 1), 1.0, 0.0).astype(BF16)
    rank = dot(hit.astype(BF16), ahead)
    return jnp.where((rank == iota((8, ROWS), 0).astype(F32)) & (hit > 0.5), 1.0, 0.0)


def scan_kernel(got_ref, sent_ref, reads_ref, enter_ref, mixed_ref):
    held = sent_ref[0:128, :].astype(F32).T
    for c in range(RANKS):
        enter_ref[c, 0:STATE, :] = held
        held = held * got_ref[c, STATE:STATE + 1, :] + got_ref[c, 0:STATE, :]
    hi, lo = halves(held)
    reads = reads_ref[...].astype(BF16)
    count = 8 * STEPS
    rows = sent_ref[128:, 0:128].astype(F32) + sent_ref[128:, 128:].astype(F32)
    y = rows[0:count] + rows[count:2 * count] * (dot(reads, hi) + dot(reads, lo))
    m = y * rows[2 * count:]
    mixed_ref[...] = m
    sums = row_sums(jnp.concatenate([m * m, jnp.zeros((128 - count, 128), F32)], 0))
    for c in range(RANKS):
        enter_ref[c, STATE:, :] = sums


def row_sums(v):
    ones = jnp.ones((8, v.shape[1]), BF16)
    hi, lo = halves(v)
    return dot(ones, hi, ((1,), (1,))) + dot(ones, lo, ((1,), (1,)))


def scales(sums):
    scale = lax.rsqrt(sums * (1.0 / WIDTH) + EPSILON)
    return jnp.broadcast_to(scale, (128, 128)).T


def rows_kernel(at_ref, sums_ref, mixed_ref, gain_ref, rows_ref):
    total = sums_ref[0]
    for c in range(1, RANKS):
        total = total + sums_ref[c]
    scale = scales(total[0:1])[:8 * STEPS]
    rows_ref[...] = (mixed_ref[...] * scale * gain_ref[...]).astype(BF16)


def out_kernel(at_ref, yl_ref, car_ref, c_ref, bt_ref, er_ref, in_ref, z_ref, gain_ref, out_ref,
               spread, state, mixed):
    @pl.when(pl.program_id(0) == 0)
    def _():
        fill_expander(spread)
        for c in range(RANKS):
            state[:, c * 128:(c + 1) * 128] = in_ref[c, 0:STATE, :]

    subs = yl_ref.shape[0] // BLOCK
    scale = None
    for sub in range(subs + 1):
        span = slice(sub * BLOCK, (sub + 1) * BLOCK)
        done = slice((sub - 1) * BLOCK, sub * BLOCK)
        total = jnp.zeros((BLOCK, 128), F32)
        for q in range(WIDTH // QUAD):
            cols = slice(q * QUAD, (q + 1) * QUAD)
            if sub < subs:
                factor = spread_heads(er_ref[sub], spread[:, cols])
                held = state[:, cols]
                y = yl_ref[span, cols].astype(F32) + dot(c_ref[span, :], held.astype(BF16)) * factor
                fresh = dot(bt_ref[sub], car_ref[span, cols])
                state[:, cols] = held * factor[BLOCK - 1:BLOCK] + fresh
                m = y * silu(z_ref[span, cols].astype(F32))
                mixed[span, cols] = m
                sq = m * m
                total = total + sum(sq[:, i:i + 128] for i in range(0, QUAD, 128))
            if sub > 0:
                out_ref[done, cols] = (mixed[done, cols] * scale * gain_ref[:, cols]).astype(BF16)
        mean = jnp.sum(total, axis=1, keepdims=True) * (1.0 / WIDTH)
        scale = lax.rsqrt(mean + EPSILON)


def two_heads(at_ref, ref):
    first = at_ref[0]
    lane = iota((1, 128), 1)
    return jnp.where(lane < HEAD, ref[first], ref[first + 1])


def decode_kernel(at_ref, alog_ref, bias_ref, skip_ref, slot_ref, cache_ref, bc_ref, x_ref, dt_ref,
                  traj_ref, z_ref, m_ref, sq_ref, rows_ref, reads_ref,
                  order, held_b, held_c, sorted_c, reads, kept):
    step = pl.program_id(0)

    @pl.when(step == 0)
    def _():
        traj = jnp.broadcast_to(traj_ref[...].astype(F32), (ROWS, ROWS))
        sub, lane = iota((ROWS, ROWS), 0), iota((ROWS, ROWS), 1)
        rank = jnp.sum(jnp.where((traj == traj.T) & (sub < lane), 1.0, 0.0), axis=0, keepdims=True)
        place = traj_ref[...].astype(F32) * 4.0 + rank
        order[...] = jnp.where(sub.astype(F32) == place, 1.0, 0.0).astype(BF16)

    shape = (96, 512)
    out, line = iota(shape, 0), iota(shape, 1)
    group = jnp.where(out < 64, at_ref[1], at_ref[2])
    wanted = (out % 32) * 16 + jnp.where(out < 32, 0, 8) + group
    pick = jnp.where(line == wanted, 1.0, 0.0).astype(BF16)
    prefill_c = []
    for g in range(ROWS // 32):
        got = dot(pick, bc_ref[g * 512:(g + 1) * 512, :]).astype(BF16)
        held_b[step, g * 32:(g + 1) * 32, :] = got[0:32]
        held_c[step, g * 32:(g + 1) * 32, :] = got[32:64]
        prefill_c.append(got[64:96])
    sorted_c[step] = dot(order[...], held_c[step]).astype(BF16)
    chosen = chosen_rows(traj_ref[...]).astype(BF16)
    reads_ref[...] = dot(chosen, jnp.concatenate(prefill_c, 0))

    @pl.when(step == STEPS - 1)
    def _():
        for g in range(ROWS // 16):
            lhs = jnp.concatenate([sorted_c[k, g * 16:(g + 1) * 16, :] for k in range(STEPS)], 0)
            row = iota((16 * STEPS, 128), 0) % 16 // 4
            out = jnp.zeros((16 * STEPS, 128), F32)
            for i in range(4):
                if g == 0 and i == 0:
                    continue
                got = dot(lhs, cache_ref[slot_ref[4 * g + i]], ((1,), (1,)))
                out = jnp.where(row == i, got, out)
            for k in range(STEPS):
                reads[k, g * 16:(g + 1) * 16, :] = out[k * 16:(k + 1) * 16]

        rate = jnp.exp(two_heads(at_ref, alog_ref)) * (-LOG2E)
        bias = two_heads(at_ref, bias_ref)
        skip = two_heads(at_ref, skip_ref)
        upper = iota((128, ROWS), 0) < HEAD
        sq_ref[...] = jnp.zeros_like(sq_ref)
        total = jnp.ones((ROWS, 128), F32)
        pushed = []
        for k in range(STEPS):
            raw = dt_ref[k]
            dt = softplus(jnp.where(upper, raw[0:1, :], raw[1:2, :]).T + bias)
            x_now = x_ref[k].astype(F32)
            decay = jnp.exp2(dt * rate)
            total = total * decay
            pushed = [p * decay for p in pushed] + [dt * x_now]
            hi, lo = halves(reads[k])
            back = dot(order[...], hi, ((0,), (0,))) + dot(order[...], lo, ((0,), (0,)))
            y = total * back + skip * x_now
            c_now = held_c[k].astype(F32)
            for j in range(k + 1):
                met = jnp.sum(held_b[j].astype(F32) * c_now, axis=1, keepdims=True)
                y = y + pushed[j] * met
            gate = silu(z_ref[k].astype(F32))
            m = y * gate
            m_ref[k] = m
            sq_ref[k:k + 1, :] = row_sums(m * m)[0:1]
            for i, part in enumerate((y, total, gate)):
                hi, lo = halves(part)
                at = 8 * (STEPS * i + k)
                kept[at:at + 8, :] = dot(chosen, hi) + dot(chosen, lo)
        rows_ref[...] = pair_halves(kept[...])


def norm_kernel(at_ref, m_ref, sq_ref, traj_ref, gain_ref, out_ref, chosen_ref):
    chosen = chosen_rows(traj_ref[...])
    chosen_ref[...] = chosen
    first = dot(chosen.astype(BF16), jnp.ones((8, 128), BF16), ((0,), (0,))) > 0.5
    for k in range(STEPS):
        out = m_ref[k] * scales(sq_ref[k:k + 1, :]) * gain_ref[...]
        out_ref[k] = jnp.where(first, 0.0, out).astype(BF16)


def patch_kernel(rest_ref, rows_ref, chosen_ref, out_ref):
    chosen = chosen_ref[...].astype(BF16)
    for k in range(STEPS):
        rows = dot(chosen, rows_ref[k * 8:(k + 1) * 8, :].astype(BF16), ((0,), (0,)))
        out_ref[k] = (rest_ref[k].astype(F32) + rows).astype(BF16)


def full(shape):
    return pl.BlockSpec(shape, lambda *_: (0,) * len(shape))


def far(x):
    return pltpu.with_memory_space_constraint(x, pltpu.HBM)


def params(mib=24):
    return pltpu.CompilerParams(vmem_limit_bytes=mib * 2**20)


def cost(flops, nbytes):
    return pl.CostEstimate(flops=flops, bytes_accessed=nbytes, transcendentals=0)


def block_rows(width):
    return pl.BlockSpec((BLOCK, width), lambda b, *_: (b, 0))


def block_times():
    return pl.BlockSpec((1, 2 * SPAN, BLOCK), lambda b, *_: (b, 0, 0))


def prep_call(here, x, *rest):
    tokens = x.shape[0]
    blocks = tokens // BLOCK
    rows = pl.BlockSpec((SUBS * BLOCK, WIDTH), lambda b, *_: (b, 0))
    shapes = [((tokens, WIDTH), BF16), ((tokens, WIDTH), BF16), ((tokens, 2 * STATE), BF16),
              ((blocks, STATE, BLOCK), BF16), ((blocks, 2 * SPAN, BLOCK), F32),
              ((blocks, BLOCK, 2 * SPAN), BF16), ((RANKS, STATE + 8, 128), F32)]
    return pl.pallas_call(
        prep_kernel,
        grid_spec=pltpu.PrefetchScalarGridSpec(
            num_scalar_prefetch=1,
            grid=(blocks // SUBS,),
            in_specs=[rows, full((tokens, 2 * STATE)), full((3, WIDTH + 2 * STATE)),
                      full((SPAN, tokens)), *[full((1, HEADS))] * 3, full((4, WIDTH)),
                      full((WIDTH // 128, 128)), full((4, 2, STATE)), full((2, STATE))],
            out_specs=[rows, rows] + [full(shape) for shape, _ in shapes[2:]],
            scratch_shapes=[pltpu.VMEM((8, WIDTH), F32), pltpu.VMEM((STATE, WIDTH), F32),
                            pltpu.VMEM((2 * SPAN, WIDTH), BF16), pltpu.VMEM((8, WIDTH), F32),
                            pltpu.VMEM((8, 2 * STATE), F32),
                            pltpu.VMEM((blocks, BLOCK, SPAN), F32),
                            pltpu.VMEM((blocks + 8, WIDTH), F32)],
        ),
        out_shape=[pltpu.HBM(shape, dtype) for shape, dtype in shapes],
        compiler_params=params(),
        cost_estimate=cost(8 * 10**9, 20 * 2**20),
        name="prep",
    )(here, x, *rest)


def inner_call(here, xc, *rest):
    tokens = xc.shape[0]
    blocks = tokens // BLOCK
    rows, times, head_specs = block_rows, block_times(), [full((1, HEADS))] * 3
    return pl.pallas_call(
        inner_kernel,
        grid_spec=pltpu.PrefetchScalarGridSpec(
            num_scalar_prefetch=1,
            grid=(blocks,),
            in_specs=[rows(WIDTH), rows(2 * STATE), times, *head_specs],
            out_specs=rows(WIDTH),
            scratch_shapes=[pltpu.VMEM((8, WIDTH), F32)],
        ),
        out_shape=pltpu.HBM((tokens, WIDTH), BF16),
        compiler_params=params(),
        cost_estimate=cost(8 * 10**9, 20 * 2**20),
        name="inner",
    )(here, xc, *rest)


def gate_call(here, yl, *rest):
    tokens = yl.shape[0]
    rows = pl.BlockSpec((SUBS * BLOCK, WIDTH), lambda b, *_: (b, 0))
    return pl.pallas_call(
        out_kernel,
        grid_spec=pltpu.PrefetchScalarGridSpec(
            num_scalar_prefetch=1,
            grid=(tokens // BLOCK // SUBS,),
            in_specs=[rows, rows, pl.BlockSpec((SUBS * BLOCK, STATE), lambda b, *_: (b, 1)),
                      pl.BlockSpec((SUBS, STATE, BLOCK), lambda b, *_: (b, 0, 0)),
                      pl.BlockSpec((SUBS, BLOCK, 2 * SPAN), lambda b, *_: (b, 0, 0)),
                      full((RANKS, STATE + 8, 128)), rows,
                      pl.BlockSpec((1, WIDTH), lambda b, at: (0, at[0]))],
            out_specs=rows,
            scratch_shapes=[pltpu.VMEM((2 * SPAN, WIDTH), BF16), pltpu.VMEM((STATE, WIDTH), F32),
                            pltpu.VMEM((SUBS * BLOCK, WIDTH), F32)],
        ),
        out_shape=jax.ShapeDtypeStruct((tokens, WIDTH), BF16),
        compiler_params=params(),
        cost_estimate=cost(4 * 10**9, 16 * 2**20),
        name="gate",
    )(here, yl, *rest)


def local(x_tokens, bc_tokens, z_tokens, dt_tokens, conv_x, conv_bc, bias_x, bias_bc, a_log, dt_bias,
          d_skip, norm_gain, state_cache, traj_slot, row_traj, x_decode, bc_decode, z_decode,
          dt_decode):
    ctx_at = lax.axis_index("ctx").astype(jnp.int32)
    head_at = lax.axis_index("head").astype(jnp.int32)
    flat = ctx_at * 8 + head_at
    tokens = x_tokens.shape[0]
    vmem = pl.BlockSpec(memory_space=pltpu.VMEM)
    smem = pl.BlockSpec(memory_space=pltpu.SMEM)

    bc_flat = bc_tokens.reshape(tokens, 2 * STATE)
    edge = jnp.concatenate(
        [x_tokens[tokens - 3:], bc_tokens[tokens - 3:].reshape(3, 2 * STATE)], 1)
    edge = lax.ppermute(edge, "ctx", [(i, i + 1) for i in range(RANKS - 1)])
    owners = [(16 * g + c, 8 * c + g) for c in range(RANKS) for g in range(8)]

    traj = far(row_traj.reshape(1, ROWS))
    here = jnp.reshape(head_at, (1,))
    per_head = [far(v.reshape(1, -1)) for v in (a_log, dt_bias, d_skip)]

    xc, car, bc, bt, rdt, er, send = prep_call(
        here, far(x_tokens), bc_flat, edge, far(dt_tokens.T), *per_head, far(conv_x),
        far(bias_x.reshape(-1, 128)), far(conv_bc.reshape(4, 2, STATE)),
        far(bias_bc.reshape(2, STATE)))

    got = lax.all_to_all(send, "ctx", 0, 0)

    yl = inner_call(here, far(xc), far(bc), far(rdt), *per_head)
    got, yl = lax.optimization_barrier((got, yl))

    lines = ROWS * 16
    at = jnp.stack([flat * 2, ctx_at // 2, head_at])
    whole = full((STEPS, ROWS, 128))
    mixed, squares, rows_dec, reads = pl.pallas_call(
        decode_kernel,
        grid_spec=pltpu.PrefetchScalarGridSpec(
            num_scalar_prefetch=1,
            grid=(STEPS,),
            in_specs=[smem] * 4 + [full(state_cache.reshape(-1, 128, STATE).shape),
                                   pl.BlockSpec((lines, STATE), lambda k, *_: (k, 0)),
                                   whole, full((STEPS, 2, ROWS)), full((1, ROWS)), whole],
            out_specs=[whole, full((8, ROWS)), full((24 * STEPS, 256)),
                       pl.BlockSpec((8, STATE), lambda k, *_: (k, 0))],
            scratch_shapes=[pltpu.VMEM((ROWS, ROWS), BF16)]
            + [pltpu.VMEM((STEPS, ROWS, STATE), BF16)] * 3
            + [pltpu.VMEM((STEPS, ROWS, 128), F32), pltpu.VMEM((24 * STEPS, 128), F32)],
        ),
        out_shape=[jax.ShapeDtypeStruct((STEPS, ROWS, 128), F32),
                   jax.ShapeDtypeStruct((8, ROWS), F32),
                   jax.ShapeDtypeStruct((24 * STEPS, 256), BF16),
                   jax.ShapeDtypeStruct((8 * STEPS, STATE), F32)],
        compiler_params=params(),
        cost_estimate=cost(2 * 10**9, 6 * 2**20),
        name="decode",
    )(at, a_log, dt_bias, d_skip, traj_slot, far(state_cache.reshape(-1, 128, STATE)),
      far(bc_decode.reshape(STEPS * lines, STATE)), far(x_decode),
      far(jnp.swapaxes(dt_decode, 1, 2)), traj, far(z_decode))
    prior = state_cache[traj_slot[0]].reshape(128, STATE)
    sent = lax.ppermute(jnp.concatenate([prior, rows_dec], 0), ("ctx", "head"), owners)

    enter, first = pl.pallas_call(
        scan_kernel,
        in_specs=[vmem] * 3,
        out_specs=[vmem] * 2,
        out_shape=[pltpu.HBM((RANKS, STATE + 8, 128), F32),
                   jax.ShapeDtypeStruct((8 * STEPS, 128), F32)],
        compiler_params=params(16),
        cost_estimate=cost(10**8, 4 * 2**20),
        name="scan",
    )(got, sent, reads)
    enter = lax.all_to_all(enter, "ctx", 0, 0)

    for away in ((1, 2, 3), (4, 8, 12)):
        squares = squares + sum(
            lax.ppermute(squares, ("ctx", "head"), [(i, i ^ d) for i in range(128)]) for d in away)

    rest, chosen = pl.pallas_call(
        norm_kernel,
        grid_spec=pltpu.PrefetchScalarGridSpec(
            num_scalar_prefetch=1,
            grid=(1,),
            in_specs=[full((STEPS, ROWS, 128)), full((8, ROWS)), full((1, ROWS)),
                      pl.BlockSpec((1, 128), lambda b, at: (0, at[0]))],
            out_specs=[full((STEPS, ROWS, 128)), full((8, ROWS))],
        ),
        out_shape=[jax.ShapeDtypeStruct((STEPS, ROWS, 128), BF16),
                   jax.ShapeDtypeStruct((8, ROWS), F32)],
        compiler_params=params(),
        cost_estimate=cost(10**7, 2**19),
        name="norm",
    )(jnp.reshape(flat, (1,)), mixed, squares, traj, far(norm_gain.reshape(1, -1)))
    enter, rest = lax.optimization_barrier((enter, rest))
    first = pl.pallas_call(
        rows_kernel,
        grid_spec=pltpu.PrefetchScalarGridSpec(
            num_scalar_prefetch=1,
            grid=(1,),
            in_specs=[pl.BlockSpec((RANKS, 8, 128), lambda b, at: (0, STATE // 8, 0)),
                      full((8 * STEPS, 128)), pl.BlockSpec((1, 128), lambda b, at: (0, at[0]))],
            out_specs=full((8 * STEPS, 128)),
        ),
        out_shape=jax.ShapeDtypeStruct((8 * STEPS, 128), BF16),
        compiler_params=params(),
        cost_estimate=cost(10**7, 2**18),
        name="rows",
    )(jnp.reshape(head_at * RANKS + ctx_at, (1,)), enter, first, far(norm_gain.reshape(1, -1)))
    first = lax.ppermute(first, ("ctx", "head"), [(b, a) for a, b in owners])

    prefill_out = gate_call(here, far(yl), far(car), far(bc), far(bt), far(er), enter, far(z_tokens),
                            far(norm_gain.reshape(1, -1)))

    decode_out = pl.pallas_call(
        patch_kernel,
        in_specs=[vmem] * 3,
        out_specs=vmem,
        out_shape=jax.ShapeDtypeStruct((STEPS, ROWS, 128), BF16),
        compiler_params=params(16),
        cost_estimate=cost(10**7, 2**18),
        name="patch",
    )(rest, first, chosen)
    return (prefill_out, decode_out)


def solution(mesh):
    in_specs = (
        P("ctx", "head"),
        P("ctx", None, "head", None),
        P("ctx", "head"),
        P("ctx", "head"),
        P(None, "head"),
        P(None, None, "head", None),
        P("head"),
        P(None, "head", None),
        P(),
        P(),
        P(),
        P(),
        P(None, ("ctx", "head"), None, None),
        P(),
        P(),
        P(None, None, ("ctx", "head")),
        P(),
        P(None, None, ("ctx", "head")),
        P(None, None, ("ctx", "head")),
    )
    out_specs = (P("ctx", "head"), P(None, None, ("ctx", "head")))
    return jax.shard_map(local, mesh=mesh, in_specs=in_specs, out_specs=out_specs, check_vma=False)
```
